32 devices in a mesh: tile: 8 (over y, x, core), view: 4 (over z).
Axes of the slice: x: 2, y: 2, z: 4, core: 2. Of those that a mesh axis runs over, the one named last changes fastest.
Arguments:
- estimate: float32 [2, 112, 224, 128], P(None, 'view', 'tile'), may hold values from 0.25 to 4
- view_data: bfloat16 [4, 8, 3, 2, 58, 58, 128], P('view', 'tile'), may hold values from 0.25 to 4
- psf: float32 [6, 3, 31], replicated, may hold values from 0 to 0.5, as said below
- background: float32 [6], replicated, may hold values from 0.1 to 1
- slot_brick: int32 [4, 8, 3], P('view', 'tile'), may hold values from 0 to 7, as said below
- slot_view: int32 [4, 8, 3], P('view', 'tile'), may hold values from 0 to 5, as said below
- intersection: int32 [4, 8, 6], P('view', 'tile'), may hold values from 0 to 1, as said below
Outputs:
- updated: float32 [2, 112, 224, 128], P(None, 'view', 'tile')
The draws below stay inside these ranges and needn't reach their ends.
Inputs may be any that keep to these rules, and one draw needn't show every extreme that they name: `slot_brick`: within a group, the jobs are exactly the pairs (brick, view) that intersection marks, each once; every brick has at least one view and one brick of each group has all 6; the jobs of a group fill its workers' 3 slots exactly. `slot_view`: the view of each job, consistent with intersection. `intersection`: each brick's row has between 1 and 6 ones. `psf`: all taps are positive.
All inputs are finite; a program needn't handle non-finite values.
Results may differ from the reference program's by a relative error of at most 0.0003.
Values may be sent and summed in bfloat16 or wider, within the bound.
A program may use at most 128 MiB of HBM per device.

```python
import math
import jax
import jax.numpy as jnp
from jax import lax

C = 2
VIEWS = 6
TAPS = 31
HALO = 15
BX = 28
BY = 28
NZ = 128
SLOTS = 3
PX = 58
PY = 58
NX = 112
NY = 224
N_TILE = 8
N_VIEW = 4


def group_tables(group_key):
    bricks = N_TILE
    full_key, fill_key, order_key, perm_key = jax.random.split(group_key, 4)
    full_brick = jax.random.randint(full_key, (), 0, bricks)
    counts = jnp.where(jnp.arange(bricks) == full_brick, VIEWS, 1).astype(jnp.int32)
    extra = bricks * SLOTS - bricks - VIEWS + 1

    def add_one(index, counts):
        scores = jax.random.randint(jax.random.fold_in(fill_key, index), (bricks,), 0, 1 << 20) * bricks + jnp.arange(bricks)
        scores = jnp.where(counts < VIEWS, scores, -1)
        return counts + (jnp.arange(bricks) == jnp.argmax(scores)).astype(jnp.int32)
    counts = lax.fori_loop(0, extra, add_one, counts)

    def one_permutation(perm_piece):
        return jax.random.permutation(perm_piece, VIEWS)
    perms = jax.vmap(one_permutation)(jax.random.split(perm_key, bricks))
    ranks = jnp.argsort(perms, axis=1)
    intersection = (ranks < counts[:, None]).astype(jnp.int32)
    pairs = bricks * VIEWS
    scores = jax.random.randint(order_key, (pairs,), 0, 1 << 20) * pairs + jnp.arange(pairs)
    scores = jnp.where(intersection.reshape(pairs) > 0, scores, scores + (1 << 20) * pairs)
    order = jnp.argsort(scores)[:bricks * SLOTS]
    slot_brick = (order // VIEWS).reshape(bricks, SLOTS).astype(jnp.int32)
    slot_view = (order % VIEWS).reshape(bricks, SLOTS).astype(jnp.int32)
    return (slot_brick, slot_view, intersection)


def job_tables(key):
    group_keys = jax.random.split(jax.random.fold_in(key, 7), N_VIEW)
    return jax.vmap(group_tables)(group_keys)


def draw_slot_brick(key, part):
    return job_tables(key)[0]


def draw_slot_view(key, part):
    return job_tables(key)[1]


def draw_intersection(key, part):
    return job_tables(key)[2]


def draw_psf(key, part):
    width_key, rough_key = jax.random.split(jax.random.fold_in(key, 11))
    widths = jnp.exp(jax.random.uniform(width_key, (VIEWS, 3, 1), jnp.float32, math.log(1.5), math.log(5.0)))
    reach = (jnp.arange(TAPS) - (TAPS - 1) // 2).astype(jnp.float32)
    rough = jax.random.uniform(rough_key, (VIEWS, 3, TAPS), jnp.float32, 0.6, 1.4)
    return jnp.exp(-0.5 * (reach / widths) ** 2) * rough / (widths * 2.5066283)


def steps_of(stream_key, shape, cuts, least, largest):
    gain, own = 1.0, jax.random.fold_in(stream_key, 6)
    for dim, shards_of in cuts:
        steps = jnp.exp(jax.random.uniform(jax.random.fold_in(own, dim), (shards_of,), jnp.float32, least / len(cuts), largest / len(cuts)))
        gain = gain * jnp.repeat(steps, shape[dim] // shards_of).reshape([-1 if axis == dim else 1 for axis in range(len(shape))])
    return gain


def setup_inputs(seed: int = 0) -> dict:
    key_of = jax.random.split(jax.random.key(seed), 8)
    estimate = jnp.clip(jnp.exp(math.log(4.0) - 2.7725887 * jax.random.uniform(key_of[0], (C, NX, NY, NZ), jnp.float32) ** steps_of(key_of[0], (C, NX, NY, NZ), ((1, 4), (2, 8)), -0.2, 0.2)), 0.25, 4.0)
    view_data = jnp.clip(jnp.exp(math.log(4.0) - 2.7725887 * jax.random.uniform(key_of[1], (N_VIEW, N_TILE, SLOTS, C, PX, PY, NZ), jnp.float32) ** steps_of(key_of[1], (N_VIEW, N_TILE, SLOTS, C, PX, PY, NZ), ((0, 4), (1, 8)), -0.2, 0.2)), 0.25, 4.0).astype(jnp.bfloat16)
    psf = draw_psf(jax.random.fold_in(key_of[7], 71), 0)
    background = jnp.clip(jnp.exp(jax.random.uniform(key_of[3], (VIEWS,), jnp.float32, math.log(0.1), math.log(1.0))), 0.1, 1.0)
    slot_brick = draw_slot_brick(jax.random.fold_in(key_of[7], 71), 0)
    slot_view = draw_slot_view(jax.random.fold_in(key_of[7], 71), 0)
    intersection = draw_intersection(jax.random.fold_in(key_of[7], 71), 0)
    return {"estimate": estimate, "view_data": view_data, "psf": psf, "background": background, "slot_brick": slot_brick, "slot_view": slot_view, "intersection": intersection}


def banded(kernel_taps, order, rim_width):
    offsets = jnp.arange(order)[None, :] - jnp.arange(order)[:, None] + rim_width
    matches = offsets[:, :, None] == jnp.arange(kernel_taps.shape[0])[None, None, :]
    return jnp.sum(jnp.where(matches, kernel_taps[None, None, :], 0.0), axis=2)


def forward_blur(block, kernels, rim_width):
    band_x = banded(kernels[0], block.shape[1], rim_width)
    band_y = banded(kernels[1], block.shape[2], rim_width)
    band_z = banded(kernels[2], block.shape[3], rim_width)
    result = jnp.einsum('cxyz,wz->cxyw', block, band_z, precision=lax.Precision.HIGHEST)
    result = jnp.einsum('cxyz,vy->cxvz', result, band_y, precision=lax.Precision.HIGHEST)
    return jnp.einsum('cxyz,ux->cuyz', result, band_x, precision=lax.Precision.HIGHEST)


def backward_blur(ratio, kernels, rim_width, brick_x, brick_y):
    band_x = banded(kernels[0], ratio.shape[1], rim_width)[:, rim_width:rim_width + brick_x]
    band_y = banded(kernels[1], ratio.shape[2], rim_width)[:, rim_width:rim_width + brick_y]
    band_z = banded(kernels[2], ratio.shape[3], rim_width)
    result = jnp.einsum('cxyz,xu->cuyz', ratio, band_x, precision=lax.Precision.HIGHEST)
    result = jnp.einsum('cxyz,yv->cxvz', result, band_y, precision=lax.Precision.HIGHEST)
    return jnp.einsum('cxyz,zw->cxyw', result, band_z, precision=lax.Precision.HIGHEST)


def reference(estimate, view_data, psf, background, slot_brick, slot_view, intersection):
    est_wire = estimate.astype(jnp.bfloat16)
    padded = jnp.pad(est_wire, ((0, 0), (HALO, HALO), (HALO, HALO), (0, 0)))
    job_count = N_VIEW * N_TILE * SLOTS
    measured_all = view_data.reshape(job_count, C, PX, PY, NZ)
    groups_all = (jnp.arange(job_count) // (N_TILE * SLOTS)).astype(jnp.int32)
    bricks_all = slot_brick.reshape(job_count).astype(jnp.int32)
    views_all = slot_view.reshape(job_count).astype(jnp.int32)
    anchor = jnp.int32(0)

    def apply_job(summed, job_item):
        measured, group_index, brick_index, view_index = job_item
        start_x = (group_index * BX).astype(jnp.int32)
        start_y = (brick_index * BY).astype(jnp.int32)
        block = lax.dynamic_slice(padded, (anchor, start_x, start_y, anchor), (C, PX, PY, NZ)).astype(jnp.float32)
        kernels = lax.dynamic_index_in_dim(psf, view_index, 0, keepdims=False)
        backdrop = lax.dynamic_index_in_dim(background, view_index, 0, keepdims=False)
        predicted = forward_blur(block, kernels, HALO) + backdrop
        ratio = measured.astype(jnp.float32) / predicted
        factor = backward_blur(ratio, kernels, HALO, BX, BY)
        previous = lax.dynamic_slice(summed, (anchor, start_x, start_y, anchor), (C, BX, BY, NZ))
        summed = lax.dynamic_update_slice(summed, previous + factor, (anchor, start_x, start_y, anchor))
        return summed, None

    summed = jnp.zeros((C, NX, NY, NZ), jnp.float32)
    summed, unused = lax.scan(apply_job, summed, (measured_all, groups_all, bricks_all, views_all))
    views_seen = jnp.sum(intersection, axis=2).astype(jnp.float32)
    seen_field = jnp.repeat(jnp.repeat(views_seen, BX, axis=0), BY, axis=1)
    return estimate * summed / seen_field[None, :, :, None]
```

```python
import functools

import jax
import jax.numpy as jnp
from jax import lax
from jax.experimental import pallas as pl
from jax.experimental.pallas import tpu as pltpu
from jax.sharding import PartitionSpec as P

MESH = pl.DeviceIdType.MESH
F32 = jnp.float32
BF16 = jnp.bfloat16
ROWS = 64
HB = 16
UP = 32
PITCH1 = 72
PITCH2 = 40
VMEM = pl.BlockSpec(memory_space=pltpu.VMEM)
SMEM = pl.BlockSpec(memory_space=pltpu.SMEM)


def place(n):
    t, v = lax.axis_index("tile"), lax.axis_index("view")
    sib = t + 1 - 2 * lax.rem(t, 2)
    return t, v, sib


def same(t, step, n):
    return lax.rem(t + 2 * step + 2 * n, n)


def greet(n, nv, with_view):
    t, v, sib = place(n)
    barrier = pltpu.get_barrier_semaphore()

    def signal(tile, view):
        pl.semaphore_signal(barrier, inc=1, device_id=(tile, view), device_id_type=MESH)

    signal(sib, v)
    for k in range(1, n // 2):
        signal(same(t, k, n), v)
    peers = n // 2
    if with_view:

        @pl.when(v > 0)
        def _():
            signal(t, v - 1)

        @pl.when(v < nv - 1)
        def _():
            signal(t, v + 1)

        peers = peers + jnp.minimum(v, 1) + jnp.minimum(nv - 1 - v, 1)
    pl.semaphore_wait(barrier, peers)


class Gather:
    def __init__(self, n, nv, by, halo, wire, out, sems):
        self.n, self.nv, self.by, self.halo = n, nv, by, halo
        self.wire, self.out = wire, out
        self.sm, self.rm, self.sz, self.rz, self.ss, self.rs, self.loc = sems
        self.t, self.v, self.sib = place(n)

    def slab(self, c, b, part):
        start, size = ((HB, 2 * HB), (0, HB), (3 * HB, HB))[part]
        return self.out.at[c, pl.ds(self.halo + self.by * b, self.by), pl.ds(start, size), :]

    def copy(self, src, dst, s, r, dev):
        return pltpu.make_async_remote_copy(
            src_ref=src, dst_ref=dst, send_sem=s, recv_sem=r, device_id=dev, device_id_type=MESH
        )

    def main(self, c, k):
        return self.copy(
            self.wire.at[c],
            self.slab(c, self.t, 0),
            self.sm.at[c, k],
            self.rm.at[c, k],
            (same(self.t, k, self.n), self.v),
        )

    def to_sib(self, c, k, part):
        b = same(self.t, -k, self.n)
        src = self.wire.at[c] if (k == 0 and part == 0) else self.slab(c, b, part)
        return self.copy(
            src, self.slab(c, b, part), self.ss.at[c, k, part], self.rs.at[c, k, part], (self.sib, self.v)
        )

    def to_view(self, c, k, up):
        b = same(self.t, -k, self.n)
        first = HB if up else 0
        if k == 0:
            src = self.wire.at[c, :, pl.ds(first, HB), :]
        else:
            src = self.out.at[c, pl.ds(self.halo + self.by * b, self.by), pl.ds(HB + first, HB), :]
        side = 0 if up else 1
        return self.copy(
            src,
            self.slab(c, b, 1 if up else 2),
            self.sz.at[c, k, side],
            self.rz.at[c, k, side],
            (self.t, self.v + 1 if up else self.v - 1),
        )

    def local(self, c):
        return pltpu.make_async_copy(self.wire.at[c], self.slab(c, self.t, 0), self.loc.at[c])

    def views(self, c, k, act):
        @pl.when(self.v < self.nv - 1)
        def _():
            act(self.to_view(c, k, True))

        @pl.when(self.v > 0)
        def _():
            act(self.to_view(c, k, False))

    def zeros(self):
        count = self.out.shape[1]
        last = self.halo + self.by * self.n

        def clear(where):
            self.out[where] = jnp.zeros(self.out.at[where].shape, BF16)

        def edge(i, _):
            for c in range(2):
                self.out[c, pl.ds(i, 1)] = jnp.zeros((1,) + self.out.shape[2:], BF16)
            return 0

        lax.fori_loop(0, self.halo, edge, 0)
        lax.fori_loop(last, count, edge, 0)

        def rows(start):
            def body(i, _):
                for c in range(2):
                    self.out[c, pl.ds(i, 1), pl.ds(start, HB), :] = jnp.zeros((1, HB, 128), BF16)
                return 0

            lax.fori_loop(self.halo, last, body, 0)

        @pl.when(self.v == 0)
        def _():
            rows(0)

        @pl.when(self.v == self.nv - 1)
        def _():
            rows(3 * HB)

    def begin(self, c):
        for k in range(1, self.n // 2):
            self.main(c, k).start()
        self.views(c, 0, lambda d: d.start())
        self.to_sib(c, 0, 0).start()
        self.local(c).start()

    def forward(self, c):
        for k in range(1, self.n // 2):
            self.main(c, k).wait_recv()
            self.views(c, k, lambda d: d.start())
            self.to_sib(c, k, 0).start()

        def side(k, part, when):
            @pl.when(when)
            def _():
                self.to_view(c, k, part == 1).wait_recv()
                self.to_sib(c, k, part).start()

        for k in range(self.n // 2):
            side(k, 1, self.v > 0)
            side(k, 2, self.v < self.nv - 1)

    def arrive(self, c):
        self.local(c).wait()
        for k in range(self.n // 2):
            self.to_sib(c, k, 0).wait_recv()

            @pl.when(self.v > 0)
            def _():
                self.to_sib(c, k, 1).wait_recv()

            @pl.when(self.v < self.nv - 1)
            def _():
                self.to_sib(c, k, 2).wait_recv()

    def finish(self, c):
        for k in range(self.n // 2):
            if k:
                self.main(c, k).wait_send()
            self.views(c, k, lambda d: d.wait_send())
            self.to_sib(c, k, 0).wait_send()

            @pl.when(self.v > 0)
            def _():
                self.to_sib(c, k, 1).wait_send()

            @pl.when(self.v < self.nv - 1)
            def _():
                self.to_sib(c, k, 2).wait_send()


def gather_sems(n):
    q = n // 2
    dma = pltpu.SemaphoreType.DMA
    return [dma((2, q)), dma((2, q)), dma((2, q, 2)), dma((2, q, 2)), dma((2, q, 3)), dma((2, q, 3)), dma((2,))]


def gather_kernel(n, nv, by, halo, wire, out, *sems):
    g = Gather(n, nv, by, halo, wire, out, sems)
    greet(n, nv, True)
    g.begin(0)
    g.begin(1)
    g.zeros()
    for c in range(2):
        g.forward(c)
    for c in range(2):
        g.arrive(c)
        g.finish(c)


def iota(shape, dim):
    return lax.broadcasted_iota(jnp.int32, shape, dim)


def split(x):
    hi = x.astype(BF16)
    return hi, (x - hi.astype(F32)).astype(BF16)


def band(tap, count, index, valid):
    index = jnp.where(valid, index, -1)
    total = jnp.zeros(index.shape, F32)
    for k in range(count):
        total = jnp.where(index == k, tap(k), total)
    return total


def build_bands(tap, dims, mats):
    fx, fy, cx, cy, fz, cz = mats
    taps, halo, bx, by, nz = dims
    px, py = bx + 2 * halo, by + 2 * halo

    def pieces(value, low):
        hi, lo = split(value)
        return jnp.where(low, lo.astype(F32), hi.astype(F32)).astype(BF16)

    p, col = iota((ROWS, 3 * ROWS), 0), iota((ROWS, 3 * ROWS), 1)
    low = (col >= ROWS) & (col < 2 * ROWS)
    r = jnp.where(col >= 2 * ROWS, col - 2 * ROWS, jnp.where(col >= ROWS, col - ROWS, col))
    gap = 2 * HB - (bx - HB) + HB
    x = jnp.where(r < 2 * HB, r - HB, r - gap + HB)
    fresh = (r < 2 * HB) | (x >= HB)
    q = x + halo
    valid = fresh & (q >= 0) & (q < px) & (p < px)
    fx[...] = pieces(band(lambda k: tap(0, k), taps, q - p + halo, valid), low)
    fy[...] = pieces(band(lambda k: tap(1, k), taps, r - p + halo, (r < py) & (p < py)), low)
    p, r, low = p[:UP], r[:UP], low[:UP]
    cx[...] = pieces(band(lambda k: tap(0, k), taps, p - r + 2 * halo, (r < px) & (p < bx)), low)
    cy[...] = pieces(band(lambda k: tap(1, k), taps, p - r + 2 * halo, (r < py) & (p < by)), low)
    row, w = iota((2 * nz, nz), 0), iota((2 * nz, nz), 1)
    z = jnp.where(row >= nz, row - nz, row)
    fz[...] = pieces(band(lambda k: tap(2, k), taps, z - w + halo, w < nz), row >= nz)
    back = band(lambda k: tap(2, k), taps, w - z + halo, w < nz)
    hi, lo = split(back)
    cz[...] = jnp.concatenate([hi, lo], axis=1)


def stack(a, b):
    ah, al = split(a)
    bh, bl = split(b)
    hi = jnp.concatenate([ah, bh], axis=1)
    lo = jnp.concatenate([al, bl], axis=1)
    return jnp.concatenate([hi, hi, lo], axis=0)


def dot(a, b):
    return jnp.dot(a, b, preferred_element_type=F32)


def job(block, view, backdrop, dims, mats, s1, s2, s3, emit):
    fx, fy, cx, cy, fz, cz = mats
    taps, halo, bx, by, nz = dims
    px, py = bx + 2 * halo, by + 2 * halo
    chunk = 8

    def first(i, _):
        e = block(i * chunk, chunk).reshape(chunk * ROWS, nz)
        t = dot(jnp.concatenate([e, e], axis=1), fz[...])
        for j in range(0, chunk, 2):
            a, b = t[j * ROWS : (j + 1) * ROWS], t[(j + 1) * ROWS : (j + 2) * ROWS]
            u = dot(fx[...], stack(a, b))
            y = i * chunk + j
            s1[pl.ds(pl.multiple_of(y * PITCH1, 8), ROWS), :] = u[:, :nz]
            s1[pl.ds(pl.multiple_of((y + 1) * PITCH1, 8), ROWS), :] = u[:, nz:]
        return 0

    lax.fori_loop(0, ROWS // chunk, first, 0)

    def second(i, _):
        x = 2 * i
        a = s1[pl.ds(x, ROWS, PITCH1), :]
        b = s1[pl.ds(x + 1, ROWS, PITCH1), :]
        predicted = dot(fy[...], stack(a, b)) + backdrop
        pad = jnp.zeros((ROWS - py, nz), F32)
        va = jnp.concatenate([view(x).astype(F32), pad], axis=0)
        vb = jnp.concatenate([view(x + 1).astype(F32), pad], axis=0)
        f = dot(cy[...], stack(va / predicted[:, :nz], vb / predicted[:, nz:]))
        s2[pl.ds(pl.multiple_of(x * PITCH2, 8), UP), :] = f[:, :nz]
        s2[pl.ds(pl.multiple_of((x + 1) * PITCH2, 8), UP), :] = f[:, nz:]
        return 0

    lax.fori_loop(0, px // 2, second, 0)

    def third(i, _):
        y = 2 * i
        a = s2[pl.ds(y, ROWS, PITCH2), :]
        b = s2[pl.ds(y + 1, ROWS, PITCH2), :]
        f = dot(cx[...], stack(a, b))
        s3[pl.ds(pl.multiple_of(y * UP, 8), UP), :] = f[:, :nz]
        s3[pl.ds(pl.multiple_of((y + 1) * UP, 8), UP), :] = f[:, nz:]
        return 0

    lax.fori_loop(0, by // 2, third, 0)
    piece = by * UP // 4

    def fourth(i, _):
        rows = pl.ds(pl.multiple_of(i * piece, 8), piece)
        hi, lo = split(s3[rows, :])
        out = dot(jnp.concatenate([hi, lo], axis=1), cz[...])
        emit(rows, out[:, :nz] + out[:, nz:])
        return 0

    lax.fori_loop(0, 4, fourth, 0)


def job_scratch(by, nz):
    return [
        pltpu.VMEM((ROWS, 3 * ROWS), BF16),
        pltpu.VMEM((ROWS, 3 * ROWS), BF16),
        pltpu.VMEM((UP, 3 * ROWS), BF16),
        pltpu.VMEM((UP, 3 * ROWS), BF16),
        pltpu.VMEM((2 * nz, nz), BF16),
        pltpu.VMEM((2 * nz, 2 * nz), BF16),
        pltpu.VMEM((ROWS * PITCH1, nz), F32),
        pltpu.VMEM((ROWS * PITCH2, nz), F32),
        pltpu.VMEM((by * UP, nz), F32),
    ]


def jobs_kernel(n, dims, gathered, views, psf, background, bricks, slot_views, contrib, *scratch):
    mats, (s1, s2, s3) = scratch[:6], scratch[6:]
    taps, halo, bx, by, nz = dims
    s, c = pl.program_id(0), pl.program_id(1)
    brick, view = bricks[s], slot_views[s]

    @pl.when((s == 0) & (c == 0))
    def _():
        s2[...] = jnp.zeros_like(s2)

    @pl.when(c == 0)
    def _():
        build_bands(lambda a, k: psf[(view * 3 + a) * taps + k], dims, mats)

    def block(y, count):
        return gathered[c, pl.ds(brick * by + y, count)]

    def emit(rows, value):
        @pl.when(s == 0)
        def _():
            for o in range(n):
                contrib[o, c, rows, :] = jnp.where(brick == o, value, 0.0)

        @pl.when(s > 0)
        def _():
            contrib[brick, c, rows, :] += value

    job(block, lambda x: views[0, 0, x], background[view], dims, mats, s1, s2, s3, emit)


class Scatter:
    def __init__(self, n, by, nz, contrib, rx1, code, scale, code_in, scale_in, sems):
        self.n, self.nz, self.rows = n, nz, by * UP
        self.contrib, self.rx1 = contrib, rx1
        self.code, self.scale, self.code_in, self.scale_in = code, scale, code_in, scale_in
        self.s1, self.r1, self.s2, self.r2 = sems
        self.t, self.v, self.sib = place(n)

    def pair(self, c, j):
        return pltpu.make_async_remote_copy(
            src_ref=self.contrib.at[same(self.sib, j, self.n), c],
            dst_ref=self.rx1.at[j, c],
            send_sem=self.s1.at[j, c],
            recv_sem=self.r1.at[j, c],
            device_id=(self.sib, self.v),
            device_id_type=MESH,
        )

    def chip(self, c, j, kind):
        src, dst = ((self.code, self.code_in), (self.scale, self.scale_in))[kind]
        return pltpu.make_async_remote_copy(
            src_ref=src.at[j, c],
            dst_ref=dst.at[j, c],
            send_sem=self.s2.at[j, c, kind],
            recv_sem=self.r2.at[j, c, kind],
            device_id=(same(self.t, j, self.n), self.v),
            device_id_type=MESH,
        )

    def order(self):
        return list(range(1, self.n // 2)) + [0]

    def begin(self, c):
        for j in self.order():
            self.pair(c, j).start()

    def send(self, c):
        piece = 128
        for j in range(1, self.n // 2):
            self.pair(c, j).wait_recv()
            o = same(self.t, j, self.n)

            def add(i, top):
                rows = pl.ds(pl.multiple_of(i * piece, 8), piece)
                value = self.contrib[o, c, rows, :] + self.rx1[j, c, rows, :]
                self.rx1[j, c, rows, :] = value
                return jnp.maximum(top, jnp.max(value.reshape(piece // 8, 8, self.nz), axis=0))

            top = lax.fori_loop(0, self.rows // piece, add, jnp.zeros((8, self.nz), F32))
            top = jnp.max(top, axis=0, keepdims=True)
            top = jnp.where(top > 0.0, top, 1.0)
            self.scale[j, c] = jnp.broadcast_to(top, (8, self.nz))
            gain = 1.0 / top

            def pack(i, _):
                rows = pl.ds(pl.multiple_of(i * piece, 16), piece)
                level = jnp.minimum(self.rx1[j, c, rows, :] * gain * 65535.0, 65535.0)
                whole = jnp.round(level).astype(jnp.int32) - 32768
                self.code[j, c, rows, :] = whole.astype(jnp.int16)
                return 0

            lax.fori_loop(0, self.rows // piece, pack, 0)
            self.chip(c, j, 0).start()
            self.chip(c, j, 1).start()

    def total(self, c):
        piece = 128
        q = self.n // 2
        self.pair(c, 0).wait_recv()
        for j in range(1, q):
            self.chip(c, j, 0).wait_recv()
            self.chip(c, j, 1).wait_recv()

        def add(i, _):
            rows = pl.ds(pl.multiple_of(i * piece, 16), piece)
            value = self.contrib[self.t, c, rows, :] + self.rx1[0, c, rows, :]
            for j in range(1, q):
                level = self.code_in[j, c, rows, :].astype(jnp.int32).astype(F32) + 32768.0
                value = value + level * (self.scale_in[j, c, 0:1, :] * (1.0 / 65535.0))
            self.rx1[0, c, rows, :] = value
            return 0

        lax.fori_loop(0, self.rows // piece, add, 0)

    def finish(self, c):
        for j in range(self.n // 2):
            self.pair(c, j).wait_send()
            if j:
                self.chip(c, j, 0).wait_send()
                self.chip(c, j, 1).wait_send()


def scatter_scratch(n, by, nz):
    q, rows = n // 2, by * UP
    dma = pltpu.SemaphoreType.DMA
    return [
        pltpu.VMEM((q, 2, rows, nz), F32),
        pltpu.VMEM((q, 2, rows, nz), jnp.int16),
        pltpu.VMEM((q, 2, 8, nz), F32),
        pltpu.VMEM((q, 2, rows, nz), jnp.int16),
        pltpu.VMEM((q, 2, 8, nz), F32),
        dma((q, 2)),
        dma((q, 2)),
        dma((q, 2, 2)),
        dma((q, 2, 2)),
    ]


def update(c, estimate, out, total, seen):
    bx, by = estimate.shape[1:3]

    def body(u, _):
        out[c, u] = estimate[c, u] * total[pl.ds(u, by, UP), :] / seen
        return 0

    lax.fori_loop(0, bx, body, 0)


def scatter_kernel(n, nv, contrib, estimate, seen_ref, out, rx1, code, scale, code_in, scale_in, *rest):
    by, nz = estimate.shape[2:]
    sems, final = rest[:4], rest[4]
    s = Scatter(n, by, nz, contrib, rx1, code, scale, code_in, scale_in, sems)
    greet(n, nv, False)
    s.begin(0)
    s.begin(1)
    seen = seen_ref[0]
    for c in range(2):
        s.send(c)
    for c in range(2):
        s.total(c)

        def move(i, _):
            rows = pl.ds(pl.multiple_of(i * 128, 8), 128)
            final[rows, :] = rx1[0, c, rows, :]
            return 0

        lax.fori_loop(0, by * UP // 128, move, 0)
        update(c, estimate, out, final, seen)
        s.finish(c)


def on_device(n, nv, estimate, view_data, psf, background, slot_brick, slot_view, intersection):
    channels, bx, by, nz = estimate.shape
    taps = psf.shape[2]
    halo = taps // 2
    dims = (taps, halo, bx, by, nz)
    slots, px, py = slot_brick.shape[2], bx + 2 * halo, by + 2 * halo
    est_wire = jnp.swapaxes(estimate.astype(BF16), 1, 2)
    wire = jnp.concatenate([est_wire[:, :, :HB], est_wire[:, :, bx - HB :]], axis=2)
    count = 2 * halo + by * n + ROWS - py
    limit = 56 * 1024 * 1024
    gathered = pl.pallas_call(
        functools.partial(gather_kernel, n, nv, by, halo),
        out_shape=jax.ShapeDtypeStruct((channels, count, ROWS, nz), BF16),
        in_specs=[VMEM],
        out_specs=VMEM,
        scratch_shapes=gather_sems(n),
        compiler_params=pltpu.CompilerParams(collective_id=0, has_side_effects=True, vmem_limit_bytes=limit),
    )(wire)
    whole = lambda *shape: pl.BlockSpec(shape, lambda s, c: (0,) * len(shape))
    contrib = pl.pallas_call(
        functools.partial(jobs_kernel, n, dims),
        grid=(slots, channels),
        out_shape=jax.ShapeDtypeStruct((n, channels, by * UP, nz), F32),
        in_specs=[
            whole(channels, count, ROWS, nz),
            pl.BlockSpec((1, 1, px, py, nz), lambda s, c: (s, c, 0, 0, 0)),
            SMEM,
            SMEM,
            SMEM,
            SMEM,
        ],
        out_specs=whole(n, channels, by * UP, nz),
        scratch_shapes=job_scratch(by, nz),
        compiler_params=pltpu.CompilerParams(vmem_limit_bytes=limit),
    )(gathered, view_data[0, 0], psf.reshape(-1), background, slot_brick[0, 0], slot_view[0, 0])
    seen = jnp.sum(intersection[0, 0]).astype(F32).reshape(1)
    return pl.pallas_call(
        functools.partial(scatter_kernel, n, nv),
        out_shape=jax.ShapeDtypeStruct(estimate.shape, F32),
        in_specs=[VMEM, VMEM, SMEM],
        out_specs=VMEM,
        scratch_shapes=scatter_scratch(n, by, nz) + [pltpu.VMEM((by * UP, nz), F32)],
        compiler_params=pltpu.CompilerParams(collective_id=1, has_side_effects=True, vmem_limit_bytes=limit),
    )(contrib, estimate, seen)


def solution(mesh):
    placed = (
        P(None, "view", "tile", None),
        P("view", "tile", None, None, None, None, None),
        P(),
        P(),
        P("view", "tile", None),
        P("view", "tile", None),
        P("view", "tile", None),
    )
    return jax.shard_map(
        functools.partial(on_device, mesh.shape["tile"], mesh.shape["view"]),
        mesh=mesh,
        in_specs=placed,
        out_specs=P(None, "view", "tile", None),
        check_vma=False,
    )
```

```python
import functools

import jax
import jax.numpy as jnp
from jax import lax
from jax.experimental import pallas as pl
from jax.experimental.pallas import tpu as pltpu
from jax.sharding import PartitionSpec as P

MESH = pl.DeviceIdType.MESH
F32 = jnp.float32
BF16 = jnp.bfloat16
ROWS = 64
HB = 16
UP = 32
PITCH1 = 72
PITCH2 = 40
VMEM = pl.BlockSpec(memory_space=pltpu.VMEM)
SMEM = pl.BlockSpec(memory_space=pltpu.SMEM)


def place(n):
    t, v = lax.axis_index("tile"), lax.axis_index("view")
    sib = t + 1 - 2 * lax.rem(t, 2)
    return t, v, sib


def same(t, step, n):
    return lax.rem(t + 2 * step + 2 * n, n)


def greet(n, nv, with_view):
    t, v, sib = place(n)
    barrier = pltpu.get_barrier_semaphore()

    def signal(tile, view):
        pl.semaphore_signal(barrier, inc=1, device_id=(tile, view), device_id_type=MESH)

    signal(sib, v)
    for k in range(1, n // 2):
        signal(same(t, k, n), v)
    peers = n // 2
    if with_view:

        @pl.when(v > 0)
        def _():
            signal(t, v - 1)

        @pl.when(v < nv - 1)
        def _():
            signal(t, v + 1)

        peers = peers + jnp.minimum(v, 1) + jnp.minimum(nv - 1 - v, 1)
    pl.semaphore_wait(barrier, peers)


class Gather:
    def __init__(self, n, nv, by, halo, wire, out, sems):
        self.n, self.nv, self.by, self.halo = n, nv, by, halo
        self.wire, self.out = wire, out
        self.sm, self.rm, self.sz, self.rz, self.ss, self.rs, self.loc = sems
        self.t, self.v, self.sib = place(n)

    def slab(self, c, b, part):
        start, size = ((HB, 2 * HB), (0, HB), (3 * HB, HB))[part]
        return self.out.at[c, pl.ds(self.halo + self.by * b, self.by), pl.ds(start, size), :]

    def copy(self, src, dst, s, r, dev):
        return pltpu.make_async_remote_copy(
            src_ref=src, dst_ref=dst, send_sem=s, recv_sem=r, device_id=dev, device_id_type=MESH
        )

    def main(self, c, k):
        return self.copy(
            self.wire.at[c],
            self.slab(c, self.t, 0),
            self.sm.at[c, k],
            self.rm.at[c, k],
            (same(self.t, k, self.n), self.v),
        )

    def to_sib(self, c, k, part):
        b = same(self.t, -k, self.n)
        src = self.wire.at[c] if (k == 0 and part == 0) else self.slab(c, b, part)
        return self.copy(
            src, self.slab(c, b, part), self.ss.at[c, k, part], self.rs.at[c, k, part], (self.sib, self.v)
        )

    def to_view(self, c, k, up):
        b = same(self.t, -k, self.n)
        first = HB if up else 0
        if k == 0:
            src = self.wire.at[c, :, pl.ds(first, HB), :]
        else:
            src = self.out.at[c, pl.ds(self.halo + self.by * b, self.by), pl.ds(HB + first, HB), :]
        side = 0 if up else 1
        return self.copy(
            src,
            self.slab(c, b, 1 if up else 2),
            self.sz.at[c, k, side],
            self.rz.at[c, k, side],
            (self.t, self.v + 1 if up else self.v - 1),
        )

    def local(self, c):
        return pltpu.make_async_copy(self.wire.at[c], self.slab(c, self.t, 0), self.loc.at[c])

    def views(self, c, k, act):
        @pl.when(self.v < self.nv - 1)
        def _():
            act(self.to_view(c, k, True))

        @pl.when(self.v > 0)
        def _():
            act(self.to_view(c, k, False))

    def zeros(self):
        count = self.out.shape[1]
        last = self.halo + self.by * self.n

        def clear(where):
            self.out[where] = jnp.zeros(self.out.at[where].shape, BF16)

        def edge(i, _):
            for c in range(2):
                self.out[c, pl.ds(i, 1)] = jnp.zeros((1,) + self.out.shape[2:], BF16)
            return 0

        lax.fori_loop(0, self.halo, edge, 0)
        lax.fori_loop(last, count, edge, 0)

        def rows(start):
            def body(i, _):
                for c in range(2):
                    self.out[c, pl.ds(i, 1), pl.ds(start, HB), :] = jnp.zeros((1, HB, 128), BF16)
                return 0

            lax.fori_loop(self.halo, last, body, 0)

        @pl.when(self.v == 0)
        def _():
            rows(0)

        @pl.when(self.v == self.nv - 1)
        def _():
            rows(3 * HB)

    def begin(self, c):
        for k in range(1, self.n // 2):
            self.main(c, k).start()
        self.views(c, 0, lambda d: d.start())
        self.to_sib(c, 0, 0).start()
        self.local(c).start()

    def forward(self, c):
        for k in range(1, self.n // 2):
            self.main(c, k).wait_recv()
            self.views(c, k, lambda d: d.start())
            self.to_sib(c, k, 0).start()

        def side(k, part, when):
            @pl.when(when)
            def _():
                self.to_view(c, k, part == 1).wait_recv()
                self.to_sib(c, k, part).start()

        for k in range(self.n // 2):
            side(k, 1, self.v > 0)
            side(k, 2, self.v < self.nv - 1)

    def arrive(self, c):
        self.local(c).wait()
        for k in range(self.n // 2):
            self.to_sib(c, k, 0).wait_recv()

            @pl.when(self.v > 0)
            def _():
                self.to_sib(c, k, 1).wait_recv()

            @pl.when(self.v < self.nv - 1)
            def _():
                self.to_sib(c, k, 2).wait_recv()

    def finish(self, c):
        for k in range(self.n // 2):
            if k:
                self.main(c, k).wait_send()
            self.views(c, k, lambda d: d.wait_send())
            self.to_sib(c, k, 0).wait_send()

            @pl.when(self.v > 0)
            def _():
                self.to_sib(c, k, 1).wait_send()

            @pl.when(self.v < self.nv - 1)
            def _():
                self.to_sib(c, k, 2).wait_send()


def gather_sems(n):
    q = n // 2
    dma = pltpu.SemaphoreType.DMA
    return [dma((2, q)), dma((2, q)), dma((2, q, 2)), dma((2, q, 2)), dma((2, q, 3)), dma((2, q, 3)), dma((2,))]


def gather_kernel(n, nv, by, halo, wire, out, *sems):
    g = Gather(n, nv, by, halo, wire, out, sems)
    greet(n, nv, True)
    g.begin(0)
    g.begin(1)
    g.zeros()
    for c in range(2):
        g.forward(c)
    for c in range(2):
        g.arrive(c)
        g.finish(c)


def iota(shape, dim):
    return lax.broadcasted_iota(jnp.int32, shape, dim)


def split(x):
    hi = x.astype(BF16)
    return hi, (x - hi.astype(F32)).astype(BF16)


def band(tap, count, index, valid):
    index = jnp.where(valid, index, -1)
    total = jnp.zeros(index.shape, F32)
    for k in range(count):
        total = jnp.where(index == k, tap(k), total)
    return total


def build_bands(tap, dims, mats):
    fx, fy, cx, cy, fz, cz = mats
    taps, halo, bx, by, nz = dims
    px, py = bx + 2 * halo, by + 2 * halo

    def pieces(value, low):
        hi, lo = split(value)
        return jnp.where(low, lo.astype(F32), hi.astype(F32)).astype(BF16)

    p, col = iota((ROWS, 3 * ROWS), 0), iota((ROWS, 3 * ROWS), 1)
    low = (col >= ROWS) & (col < 2 * ROWS)
    r = jnp.where(col >= 2 * ROWS, col - 2 * ROWS, jnp.where(col >= ROWS, col - ROWS, col))
    gap = 2 * HB - (bx - HB) + HB
    x = jnp.where(r < 2 * HB, r - HB, r - gap + HB)
    fresh = (r < 2 * HB) | (x >= HB)
    q = x + halo
    valid = fresh & (q >= 0) & (q < px) & (p < px)
    fx[...] = pieces(band(lambda k: tap(0, k), taps, q - p + halo, valid), low)
    fy[...] = pieces(band(lambda k: tap(1, k), taps, r - p + halo, (r < py) & (p < py)), low)
    p, r, low = p[:UP], r[:UP], low[:UP]
    cx[...] = pieces(band(lambda k: tap(0, k), taps, p - r + 2 * halo, (r < px) & (p < bx)), low)
    cy[...] = pieces(band(lambda k: tap(1, k), taps, p - r + 2 * halo, (r < py) & (p < by)), low)
    z, w = iota((nz, nz), 0), iota((nz, nz), 1)
    hi, lo = split(band(lambda k: tap(2, k), taps, z - w + halo, w < nz))
    fz[...] = jnp.concatenate([hi, lo], axis=0)
    hi, lo = split(band(lambda k: tap(2, k), taps, w - z + halo, w < nz))
    back = jnp.concatenate([hi, lo], axis=1)
    cz[...] = jnp.concatenate([back, back], axis=0)


def stack(a, b):
    ah, al = split(a)
    bh, bl = split(b)
    hi = jnp.concatenate([ah, bh], axis=1)
    lo = jnp.concatenate([al, bl], axis=1)
    return jnp.concatenate([hi, hi, lo], axis=0)


def dot(a, b):
    return jnp.dot(a, b, preferred_element_type=F32)


def in_groups(count, size, body):
    full = count // size
    if full:

        def step(i, _):
            body(i * size, size)
            return 0

        lax.fori_loop(0, full, step, 0)
    if count % size:
        body(full * size, count % size)


def job(block, view, backdrop, dims, mats, s1, s2, emit):
    fx, fy, cx, cy, fz, cz = mats
    taps, halo, bx, by, nz = dims
    px, py = bx + 2 * halo, by + 2 * halo

    def put(ref, line, pitch, size, value):
        ref[pl.ds(pl.multiple_of(line * pitch, 8), size), :] = value[:, :nz]
        ref[pl.ds(pl.multiple_of((line + 1) * pitch, 8), size), :] = value[:, nz:]

    def first(y, count):
        e = block(y, count).reshape(count * ROWS, nz)
        t = dot(jnp.concatenate([e, e], axis=1), fz[...])
        lines = [t[j * ROWS : (j + 1) * ROWS] for j in range(count)]
        done = [dot(fx[...], stack(lines[j], lines[j + 1])) for j in range(0, count, 2)]
        for j, u in enumerate(done):
            put(s1, y + 2 * j, PITCH1, ROWS, u)

    in_groups(ROWS, 8, first)

    def second(pair, count):
        pad = jnp.zeros((ROWS - py, nz), F32)
        done = []
        for j in range(count):
            x = 2 * (pair + j)
            a = s1[pl.ds(x, ROWS, PITCH1), :]
            b = s1[pl.ds(x + 1, ROWS, PITCH1), :]
            predicted = dot(fy[...], stack(a, b)) + backdrop
            va = jnp.concatenate([view(x).astype(F32), pad], axis=0)
            vb = jnp.concatenate([view(x + 1).astype(F32), pad], axis=0)
            done.append((va / predicted[:, :nz], vb / predicted[:, nz:]))
        done = [dot(cy[...], stack(a, b)) for a, b in done]
        for j, f in enumerate(done):
            put(s2, 2 * (pair + j), PITCH2, UP, f)

    in_groups(px // 2, 4, second)

    def third(pair, count):
        done = []
        for j in range(count):
            y = 2 * (pair + j)
            a = s2[pl.ds(y, ROWS, PITCH2), :]
            b = s2[pl.ds(y + 1, ROWS, PITCH2), :]
            done.append(dot(cx[...], stack(a, b)))
        f = jnp.concatenate([v for f in done for v in (f[:, :nz], f[:, nz:])], axis=0)
        hi, lo = split(f)
        out = dot(jnp.concatenate([hi, lo], axis=1), cz[...])
        emit(pl.ds(pl.multiple_of(pair * 2 * UP, 8), count * 2 * UP), out[:, :nz] + out[:, nz:])

    in_groups(by // 2, 7, third)


def job_scratch(by, nz):
    return [
        pltpu.VMEM((ROWS, 3 * ROWS), BF16),
        pltpu.VMEM((ROWS, 3 * ROWS), BF16),
        pltpu.VMEM((UP, 3 * ROWS), BF16),
        pltpu.VMEM((UP, 3 * ROWS), BF16),
        pltpu.VMEM((2 * nz, nz), BF16),
        pltpu.VMEM((2 * nz, 2 * nz), BF16),
        pltpu.VMEM((ROWS * PITCH1, nz), F32),
        pltpu.VMEM((ROWS * PITCH2, nz), F32),
    ]


def jobs_kernel(n, dims, gathered, views, psf, background, bricks, slot_views, contrib, *scratch):
    mats, (s1, s2) = scratch[:6], scratch[6:]
    taps, halo, bx, by, nz = dims
    s, c = pl.program_id(0), pl.program_id(1)
    brick, view = bricks[s], slot_views[s]

    @pl.when((s == 0) & (c == 0))
    def _():
        s2[...] = jnp.zeros_like(s2)

    @pl.when(c == 0)
    def _():
        build_bands(lambda a, k: psf[(view * 3 + a) * taps + k], dims, mats)

    def block(y, count):
        return gathered[c, pl.ds(brick * by + y, count)]

    def emit(rows, value):
        @pl.when(s == 0)
        def _():
            for o in range(n):
                contrib[o, c, rows, :] = jnp.where(brick == o, value, 0.0)

        @pl.when(s > 0)
        def _():
            contrib[brick, c, rows, :] += value

    job(block, lambda x: views[0, 0, x], background[view], dims, mats, s1, s2, emit)


class Scatter:
    def __init__(self, n, by, nz, contrib, rx1, code, scale, code_in, scale_in, sems):
        self.n, self.nz, self.rows = n, nz, by * UP
        self.contrib, self.rx1 = contrib, rx1
        self.code, self.scale, self.code_in, self.scale_in = code, scale, code_in, scale_in
        self.s1, self.r1, self.s2, self.r2 = sems
        self.t, self.v, self.sib = place(n)

    def pair(self, c, j):
        return pltpu.make_async_remote_copy(
            src_ref=self.contrib.at[same(self.sib, j, self.n), c],
            dst_ref=self.rx1.at[j, c],
            send_sem=self.s1.at[j, c],
            recv_sem=self.r1.at[j, c],
            device_id=(self.sib, self.v),
            device_id_type=MESH,
        )

    def chip(self, c, j, kind):
        src, dst = ((self.code, self.code_in), (self.scale, self.scale_in))[kind]
        return pltpu.make_async_remote_copy(
            src_ref=src.at[j, c],
            dst_ref=dst.at[j, c],
            send_sem=self.s2.at[j, c, kind],
            recv_sem=self.r2.at[j, c, kind],
            device_id=(same(self.t, j, self.n), self.v),
            device_id_type=MESH,
        )

    def order(self):
        return list(range(1, self.n // 2)) + [0]

    def begin(self, c):
        for j in self.order():
            self.pair(c, j).start()

    def send(self, c):
        piece = 128
        for j in range(1, self.n // 2):
            self.pair(c, j).wait_recv()
            o = same(self.t, j, self.n)

            def add(i, top):
                rows = pl.ds(pl.multiple_of(i * piece, 8), piece)
                value = self.contrib[o, c, rows, :] + self.rx1[j, c, rows, :]
                self.rx1[j, c, rows, :] = value
                return jnp.maximum(top, jnp.max(value.reshape(piece // 8, 8, self.nz), axis=0))

            top = lax.fori_loop(0, self.rows // piece, add, jnp.zeros((8, self.nz), F32))
            top = jnp.max(top, axis=0, keepdims=True)
            top = jnp.where(top > 0.0, top, 1.0)
            self.scale[j, c] = jnp.broadcast_to(top, (8, self.nz))
            gain = 1.0 / top

            def pack(i, _):
                rows = pl.ds(pl.multiple_of(i * piece, 16), piece)
                level = jnp.minimum(self.rx1[j, c, rows, :] * gain * 65535.0, 65535.0)
                whole = jnp.round(level).astype(jnp.int32) - 32768
                self.code[j, c, rows, :] = whole.astype(jnp.int16)
                return 0

            lax.fori_loop(0, self.rows // piece, pack, 0)
            self.chip(c, j, 0).start()
            self.chip(c, j, 1).start()

    def total(self, c):
        piece = 128
        q = self.n // 2
        self.pair(c, 0).wait_recv()
        for j in range(1, q):
            self.chip(c, j, 0).wait_recv()
            self.chip(c, j, 1).wait_recv()

        def add(i, _):
            rows = pl.ds(pl.multiple_of(i * piece, 16), piece)
            value = self.contrib[self.t, c, rows, :] + self.rx1[0, c, rows, :]
            for j in range(1, q):
                level = self.code_in[j, c, rows, :].astype(jnp.int32).astype(F32) + 32768.0
                value = value + level * (self.scale_in[j, c, 0:1, :] * (1.0 / 65535.0))
            self.rx1[0, c, rows, :] = value
            return 0

        lax.fori_loop(0, self.rows // piece, add, 0)

    def finish(self, c):
        for j in range(self.n // 2):
            self.pair(c, j).wait_send()
            if j:
                self.chip(c, j, 0).wait_send()
                self.chip(c, j, 1).wait_send()


def scatter_scratch(n, by, nz):
    q, rows = n // 2, by * UP
    dma = pltpu.SemaphoreType.DMA
    return [
        pltpu.VMEM((q, 2, rows, nz), F32),
        pltpu.VMEM((q, 2, rows, nz), jnp.int16),
        pltpu.VMEM((q, 2, 8, nz), F32),
        pltpu.VMEM((q, 2, rows, nz), jnp.int16),
        pltpu.VMEM((q, 2, 8, nz), F32),
        dma((q, 2)),
        dma((q, 2)),
        dma((q, 2, 2)),
        dma((q, 2, 2)),
    ]


def update(c, estimate, out, total, seen):
    bx, by = estimate.shape[1:3]

    def body(u, _):
        out[c, u] = estimate[c, u] * total[pl.ds(u, by, UP), :] / seen
        return 0

    lax.fori_loop(0, bx, body, 0)


def scatter_kernel(n, nv, contrib, estimate, seen_ref, out, rx1, code, scale, code_in, scale_in, *rest):
    by, nz = estimate.shape[2:]
    sems, final = rest[:4], rest[4]
    s = Scatter(n, by, nz, contrib, rx1, code, scale, code_in, scale_in, sems)
    greet(n, nv, False)
    s.begin(0)
    s.begin(1)
    seen = seen_ref[0]
    for c in range(2):
        s.send(c)
    for c in range(2):
        s.total(c)

        def move(i, _):
            rows = pl.ds(pl.multiple_of(i * 128, 8), 128)
            final[rows, :] = rx1[0, c, rows, :]
            return 0

        lax.fori_loop(0, by * UP // 128, move, 0)
        update(c, estimate, out, final, seen)
        s.finish(c)


def on_device(n, nv, estimate, view_data, psf, background, slot_brick, slot_view, intersection):
    channels, bx, by, nz = estimate.shape
    taps = psf.shape[2]
    halo = taps // 2
    dims = (taps, halo, bx, by, nz)
    slots, px, py = slot_brick.shape[2], bx + 2 * halo, by + 2 * halo
    est_wire = jnp.swapaxes(estimate.astype(BF16), 1, 2)
    wire = jnp.concatenate([est_wire[:, :, :HB], est_wire[:, :, bx - HB :]], axis=2)
    count = 2 * halo + by * n + ROWS - py
    limit = 56 * 1024 * 1024
    gathered = pl.pallas_call(
        functools.partial(gather_kernel, n, nv, by, halo),
        out_shape=jax.ShapeDtypeStruct((channels, count, ROWS, nz), BF16),
        in_specs=[VMEM],
        out_specs=VMEM,
        scratch_shapes=gather_sems(n),
        compiler_params=pltpu.CompilerParams(collective_id=0, has_side_effects=True, vmem_limit_bytes=limit),
    )(wire)
    whole = lambda *shape: pl.BlockSpec(shape, lambda s, c: (0,) * len(shape))
    contrib = pl.pallas_call(
        functools.partial(jobs_kernel, n, dims),
        grid=(slots, channels),
        out_shape=jax.ShapeDtypeStruct((n, channels, by * UP, nz), F32),
        in_specs=[
            whole(channels, count, ROWS, nz),
            pl.BlockSpec((1, 1, px, py, nz), lambda s, c: (s, c, 0, 0, 0)),
            SMEM,
            SMEM,
            SMEM,
            SMEM,
        ],
        out_specs=whole(n, channels, by * UP, nz),
        scratch_shapes=job_scratch(by, nz),
        compiler_params=pltpu.CompilerParams(vmem_limit_bytes=limit),
    )(gathered, view_data[0, 0], psf.reshape(-1), background, slot_brick[0, 0], slot_view[0, 0])
    seen = jnp.sum(intersection[0, 0]).astype(F32).reshape(1)
    return pl.pallas_call(
        functools.partial(scatter_kernel, n, nv),
        out_shape=jax.ShapeDtypeStruct(estimate.shape, F32),
        in_specs=[VMEM, VMEM, SMEM],
        out_specs=VMEM,
        scratch_shapes=scatter_scratch(n, by, nz) + [pltpu.VMEM((by * UP, nz), F32)],
        compiler_params=pltpu.CompilerParams(collective_id=1, has_side_effects=True, vmem_limit_bytes=limit),
    )(contrib, estimate, seen)


def solution(mesh):
    placed = (
        P(None, "view", "tile", None),
        P("view", "tile", None, None, None, None, None),
        P(),
        P(),
        P("view", "tile", None),
        P("view", "tile", None),
        P("view", "tile", None),
    )
    return jax.shard_map(
        functools.partial(on_device, mesh.shape["tile"], mesh.shape["view"]),
        mesh=mesh,
        in_specs=placed,
        out_specs=P(None, "view", "tile", None),
        check_vma=False,
    )
```

```python
import functools

import jax
import jax.numpy as jnp
from jax import lax
from jax.experimental import pallas as pl
from jax.experimental.pallas import tpu as pltpu
from jax.sharding import PartitionSpec as P

MESH = pl.DeviceIdType.MESH
F32 = jnp.float32
BF16 = jnp.bfloat16
ROWS = 64
HB = 16
UP = 32
PITCH1 = 72
PITCH2 = 40
VMEM = pl.BlockSpec(memory_space=pltpu.VMEM)
SMEM = pl.BlockSpec(memory_space=pltpu.SMEM)


def place(n):
    t, v = lax.axis_index("tile"), lax.axis_index("view")
    sib = t + 1 - 2 * lax.rem(t, 2)
    return t, v, sib


def same(t, step, n):
    return lax.rem(t + 2 * step + 2 * n, n)


def greet(n, nv, with_view):
    t, v, sib = place(n)
    barrier = pltpu.get_barrier_semaphore()

    def signal(tile, view):
        pl.semaphore_signal(barrier, inc=1, device_id=(tile, view), device_id_type=MESH)

    signal(sib, v)
    for k in range(1, n // 2):
        signal(same(t, k, n), v)
    peers = n // 2
    if with_view:

        @pl.when(v > 0)
        def _():
            signal(t, v - 1)

        @pl.when(v < nv - 1)
        def _():
            signal(t, v + 1)

        peers = peers + jnp.minimum(v, 1) + jnp.minimum(nv - 1 - v, 1)
    pl.semaphore_wait(barrier, peers)


class Gather:
    def __init__(self, n, nv, by, halo, wire, out, sems):
        self.n, self.nv, self.by, self.halo = n, nv, by, halo
        self.wire, self.out = wire, out
        self.sm, self.rm, self.sz, self.rz, self.ss, self.rs, self.loc = sems
        self.t, self.v, self.sib = place(n)

    def slab(self, c, b, part):
        start, size = ((HB, 2 * HB), (0, HB), (3 * HB, HB))[part]
        return self.out[c].at[pl.ds(self.halo + self.by * b, self.by), pl.ds(start, size), :]

    def copy(self, src, dst, s, r, dev):
        return pltpu.make_async_remote_copy(
            src_ref=src, dst_ref=dst, send_sem=s, recv_sem=r, device_id=dev, device_id_type=MESH
        )

    def main(self, c, k):
        return self.copy(
            self.wire.at[c],
            self.slab(c, self.t, 0),
            self.sm.at[c, k],
            self.rm.at[c, k],
            (same(self.t, k, self.n), self.v),
        )

    def to_sib(self, c, k, part):
        b = same(self.t, -k, self.n)
        src = self.wire.at[c] if (k == 0 and part == 0) else self.slab(c, b, part)
        return self.copy(
            src, self.slab(c, b, part), self.ss.at[c, k, part], self.rs.at[c, k, part], (self.sib, self.v)
        )

    def to_view(self, c, k, up):
        b = same(self.t, -k, self.n)
        first = HB if up else 0
        if k == 0:
            src = self.wire.at[c, :, pl.ds(first, HB), :]
        else:
            src = self.out[c].at[pl.ds(self.halo + self.by * b, self.by), pl.ds(HB + first, HB), :]
        side = 0 if up else 1
        return self.copy(
            src,
            self.slab(c, b, 1 if up else 2),
            self.sz.at[c, k, side],
            self.rz.at[c, k, side],
            (self.t, self.v + 1 if up else self.v - 1),
        )

    def local(self, c):
        return pltpu.make_async_copy(self.wire.at[c], self.slab(c, self.t, 0), self.loc.at[c])

    def views(self, c, k, act):
        @pl.when(self.v < self.nv - 1)
        def _():
            act(self.to_view(c, k, True))

        @pl.when(self.v > 0)
        def _():
            act(self.to_view(c, k, False))

    def zeros(self):
        count = self.out[0].shape[0]
        last = self.halo + self.by * self.n

        def fill(low, high, start, size):
            def body(i, _):
                for ref in self.out:
                    ref[pl.ds(i, 1), pl.ds(start, size), :] = jnp.zeros((1, size, ref.shape[2]), BF16)
                return 0

            lax.fori_loop(low, high, body, 0)

        fill(0, self.halo, 0, ROWS)
        fill(last, count, 0, ROWS)

        @pl.when(self.v == 0)
        def _():
            fill(self.halo, last, 0, HB)

        @pl.when(self.v == self.nv - 1)
        def _():
            fill(self.halo, last, 3 * HB, HB)

    def begin(self, c):
        for k in range(1, self.n // 2):
            self.main(c, k).start()
        self.views(c, 0, lambda d: d.start())
        self.to_sib(c, 0, 0).start()
        self.local(c).start()

    def forward(self, c):
        for k in range(1, self.n // 2):
            self.main(c, k).wait_recv()
            self.views(c, k, lambda d: d.start())
            self.to_sib(c, k, 0).start()

    def forward_sides(self, c):
        def side(k, part, when):
            @pl.when(when)
            def _():
                self.to_view(c, k, part == 1).wait_recv()
                self.to_sib(c, k, part).start()

        for k in range(self.n // 2):
            side(k, 1, self.v > 0)
            side(k, 2, self.v < self.nv - 1)

    def arrive(self, c):
        self.local(c).wait()
        for k in range(self.n // 2):
            self.to_sib(c, k, 0).wait_recv()

            @pl.when(self.v > 0)
            def _():
                self.to_sib(c, k, 1).wait_recv()

            @pl.when(self.v < self.nv - 1)
            def _():
                self.to_sib(c, k, 2).wait_recv()

    def finish(self, c):
        for k in range(self.n // 2):
            if k:
                self.main(c, k).wait_send()
            self.views(c, k, lambda d: d.wait_send())
            self.to_sib(c, k, 0).wait_send()

            @pl.when(self.v > 0)
            def _():
                self.to_sib(c, k, 1).wait_send()

            @pl.when(self.v < self.nv - 1)
            def _():
                self.to_sib(c, k, 2).wait_send()


def gather_sems(n):
    q = n // 2
    dma = pltpu.SemaphoreType.DMA
    return [dma((2, q)), dma((2, q)), dma((2, q, 2)), dma((2, q, 2)), dma((2, q, 3)), dma((2, q, 3)), dma((2,))]


def iota(shape, dim):
    return lax.broadcasted_iota(jnp.int32, shape, dim)


def split(x):
    hi = x.astype(BF16)
    return hi, (x - hi.astype(F32)).astype(BF16)


def band(tap, count, index, valid):
    index = jnp.where(valid, index, -1)
    total = jnp.zeros(index.shape, F32)
    for k in range(count):
        total = jnp.where(index == k, tap(k), total)
    return total


def build_bands(tap, dims, mats):
    fx, fy, cx, cy, fz, cz = mats
    taps, halo, bx, by, nz = dims
    px, py = bx + 2 * halo, by + 2 * halo

    def pieces(value, low):
        hi, lo = split(value)
        return jnp.where(low, lo.astype(F32), hi.astype(F32)).astype(BF16)

    p, col = iota((ROWS, 3 * ROWS), 0), iota((ROWS, 3 * ROWS), 1)
    low = (col >= ROWS) & (col < 2 * ROWS)
    r = jnp.where(col >= 2 * ROWS, col - 2 * ROWS, jnp.where(col >= ROWS, col - ROWS, col))
    gap = 2 * HB - (bx - HB) + HB
    x = jnp.where(r < 2 * HB, r - HB, r - gap + HB)
    fresh = (r < 2 * HB) | (x >= HB)
    q = x + halo
    valid = fresh & (q >= 0) & (q < px) & (p < px)
    fx[...] = pieces(band(lambda k: tap(0, k), taps, q - p + halo, valid), low)
    fy[...] = pieces(band(lambda k: tap(1, k), taps, r - p + halo, (r < py) & (p < py)), low)
    p, r, low = p[:UP], r[:UP], low[:UP]
    cx[...] = pieces(band(lambda k: tap(0, k), taps, p - r + 2 * halo, (r < px) & (p < bx)), low)
    cy[...] = pieces(band(lambda k: tap(1, k), taps, p - r + 2 * halo, (r < py) & (p < by)), low)
    z, w = iota((nz, nz), 0), iota((nz, nz), 1)
    hi, lo = split(band(lambda k: tap(2, k), taps, z - w + halo, w < nz))
    fz[...] = jnp.concatenate([hi, lo], axis=0)
    hi, lo = split(band(lambda k: tap(2, k), taps, w - z + halo, w < nz))
    back = jnp.concatenate([hi, lo], axis=1)
    cz[...] = jnp.concatenate([back, back], axis=0)


def stack(a, b):
    ah, al = split(a)
    bh, bl = split(b)
    hi = jnp.concatenate([ah, bh], axis=1)
    lo = jnp.concatenate([al, bl], axis=1)
    return jnp.concatenate([hi, hi, lo], axis=0)


def dot(a, b):
    return jnp.dot(a, b, preferred_element_type=F32)


def in_groups(count, size, body):
    full = count // size
    if full:

        def step(i, _):
            body(i * size, size)
            return 0

        lax.fori_loop(0, full, step, 0)
    if count % size:
        body(full * size, count % size)


def job(block, view, backdrop, dims, mats, s1, s2, emit):
    fx, fy, cx, cy, fz, cz = mats
    taps, halo, bx, by, nz = dims
    px, py = bx + 2 * halo, by + 2 * halo

    def put(ref, line, pitch, size, value):
        ref[pl.ds(pl.multiple_of(line * pitch, 8), size), :] = value[:, :nz]
        ref[pl.ds(pl.multiple_of((line + 1) * pitch, 8), size), :] = value[:, nz:]

    def first(y, count):
        e = block(y, count).reshape(count * ROWS, nz)
        t = dot(jnp.concatenate([e, e], axis=1), fz[...])
        lines = [t[j * ROWS : (j + 1) * ROWS] for j in range(count)]
        done = [dot(fx[...], stack(lines[j], lines[j + 1])) for j in range(0, count, 2)]
        for j, u in enumerate(done):
            put(s1, y + 2 * j, PITCH1, ROWS, u)

    in_groups(ROWS, 8, first)

    def second(pair, count):
        pad = jnp.zeros((ROWS - py, nz), F32)
        done = []
        for j in range(count):
            x = 2 * (pair + j)
            a = s1[pl.ds(x, ROWS, PITCH1), :]
            b = s1[pl.ds(x + 1, ROWS, PITCH1), :]
            predicted = dot(fy[...], stack(a, b)) + backdrop
            va = jnp.concatenate([view(x).astype(F32), pad], axis=0)
            vb = jnp.concatenate([view(x + 1).astype(F32), pad], axis=0)
            done.append((va / predicted[:, :nz], vb / predicted[:, nz:]))
        done = [dot(cy[...], stack(a, b)) for a, b in done]
        for j, f in enumerate(done):
            put(s2, 2 * (pair + j), PITCH2, UP, f)

    in_groups(px // 2, 4, second)

    def third(pair, count):
        done = []
        for j in range(count):
            y = 2 * (pair + j)
            a = s2[pl.ds(y, ROWS, PITCH2), :]
            b = s2[pl.ds(y + 1, ROWS, PITCH2), :]
            done.append(dot(cx[...], stack(a, b)))
        f = jnp.concatenate([v for f in done for v in (f[:, :nz], f[:, nz:])], axis=0)
        hi, lo = split(f)
        out = dot(jnp.concatenate([hi, lo], axis=1), cz[...])
        emit(pl.ds(pl.multiple_of(pair * 2 * UP, 8), count * 2 * UP), out[:, :nz] + out[:, nz:])

    in_groups(by // 2, 7, third)


def job_scratch(slots, nz):
    return [
        pltpu.VMEM((slots, ROWS, 3 * ROWS), BF16),
        pltpu.VMEM((slots, ROWS, 3 * ROWS), BF16),
        pltpu.VMEM((slots, UP, 3 * ROWS), BF16),
        pltpu.VMEM((slots, UP, 3 * ROWS), BF16),
        pltpu.VMEM((slots, 2 * nz, nz), BF16),
        pltpu.VMEM((slots, 2 * nz, 2 * nz), BF16),
        pltpu.VMEM((ROWS * PITCH1, nz), F32),
        pltpu.VMEM((ROWS * PITCH2, nz), F32),
    ]


class Scatter:
    def __init__(self, n, by, nz, bricks, factors, tx1, rx1, code, scale, code_in, scale_in, final, sems):
        self.n, self.nz, self.rows = n, nz, by * UP
        self.bricks, self.factors, self.tx1, self.rx1, self.final = bricks, factors, tx1, rx1, final
        self.code, self.scale, self.code_in, self.scale_in = code, scale, code_in, scale_in
        self.s1, self.r1, self.s2, self.r2 = sems
        self.t, self.v, self.sib = place(n)

    def own(self, c, o, rows):
        parts = [
            jnp.where(self.bricks[s] == o, self.factors[s, c, rows, :], 0.0)
            for s in range(self.factors.shape[0])
        ]
        return sum(parts[1:], parts[0])

    def loop(self, body, init=0):
        piece = 128

        def step(i, carry):
            return body(pl.ds(pl.multiple_of(i * piece, 16), piece), carry)

        return lax.fori_loop(0, self.rows // piece, step, init)

    def pair(self, c, j):
        return pltpu.make_async_remote_copy(
            src_ref=self.tx1.at[j, c],
            dst_ref=self.rx1.at[j, c],
            send_sem=self.s1.at[j, c],
            recv_sem=self.r1.at[j, c],
            device_id=(self.sib, self.v),
            device_id_type=MESH,
        )

    def chip(self, c, j, kind):
        src, dst = ((self.code, self.code_in), (self.scale, self.scale_in))[kind]
        return pltpu.make_async_remote_copy(
            src_ref=src.at[j, c],
            dst_ref=dst.at[j, c],
            send_sem=self.s2.at[j, c, kind],
            recv_sem=self.r2.at[j, c, kind],
            device_id=(same(self.t, j, self.n), self.v),
            device_id_type=MESH,
        )

    def begin(self, c):
        for j in list(range(1, self.n // 2)) + [0]:
            o = same(self.sib, j, self.n)

            def fill(rows, _):
                self.tx1[j, c, rows, :] = self.own(c, o, rows)
                return 0

            self.loop(fill)
            self.pair(c, j).start()

    def send(self, c):
        for j in range(1, self.n // 2):
            self.pair(c, j).wait_recv()
            o = same(self.t, j, self.n)

            def add(rows, top):
                value = self.own(c, o, rows) + self.rx1[j, c, rows, :]
                self.rx1[j, c, rows, :] = value
                return jnp.maximum(top, jnp.max(value.reshape(-1, 8, self.nz), axis=0))

            top = self.loop(add, jnp.zeros((8, self.nz), F32))
            top = jnp.max(top, axis=0, keepdims=True)
            top = jnp.where(top > 0.0, top, 1.0)
            self.scale[j, c] = jnp.broadcast_to(top, (8, self.nz))
            gain = 1.0 / top

            def pack(rows, _):
                level = jnp.minimum(self.rx1[j, c, rows, :] * gain * 65535.0, 65535.0)
                whole = jnp.round(level).astype(jnp.int32) - 32768
                self.code[j, c, rows, :] = whole.astype(jnp.int16)
                return 0

            self.loop(pack)
            self.chip(c, j, 0).start()
            self.chip(c, j, 1).start()

    def total(self, c):
        q = self.n // 2
        self.pair(c, 0).wait_recv()
        for j in range(1, q):
            self.chip(c, j, 0).wait_recv()
            self.chip(c, j, 1).wait_recv()

        def add(rows, _):
            value = self.own(c, self.t, rows) + self.rx1[0, c, rows, :]
            for j in range(1, q):
                level = self.code_in[j, c, rows, :].astype(jnp.int32).astype(F32) + 32768.0
                value = value + level * (self.scale_in[j, c, 0:1, :] * (1.0 / 65535.0))
            self.final[rows, :] = value
            return 0

        self.loop(add)

    def finish(self, c):
        for j in range(self.n // 2):
            self.pair(c, j).wait_send()
            if j:
                self.chip(c, j, 0).wait_send()
                self.chip(c, j, 1).wait_send()


def scatter_scratch(n, slots, by, nz):
    q, rows = n // 2, by * UP
    return [
        pltpu.VMEM((slots, 2, rows, nz), F32),
        pltpu.VMEM((q, 2, rows, nz), F32),
        pltpu.VMEM((q, 2, rows, nz), F32),
        pltpu.VMEM((q, 2, rows, nz), jnp.int16),
        pltpu.VMEM((q, 2, 8, nz), F32),
        pltpu.VMEM((q, 2, rows, nz), jnp.int16),
        pltpu.VMEM((q, 2, 8, nz), F32),
        pltpu.VMEM((rows, nz), F32),
    ]


def scatter_sems(n):
    q = n // 2
    dma = pltpu.SemaphoreType.DMA
    return [dma((q, 2)), dma((q, 2)), dma((q, 2, 2)), dma((q, 2, 2))]


def update(c, estimate, out, total, seen):
    bx, by = estimate.shape[1:3]

    def body(u, _):
        out[c, u] = estimate[c, u] * total[pl.ds(u, by, UP), :] / seen
        return 0

    lax.fori_loop(0, bx, body, 0)


def kernel(n, nv, dims, wire, estimate, views, psf, background, bricks, slot_views, crossing, out, *scratch):
    taps, halo, bx, by, nz = dims
    slots = views.shape[0]
    take = lambda count: [scratch.pop(0) for _ in range(count)]
    scratch = list(scratch)
    blocks, (seen_views, views_sem), mats, (s1, s2), parts = take(2), take(2), take(6), take(2), take(8)
    gather_all, scatter_all = take(7), take(4)
    g = Gather(n, nv, by, halo, wire, blocks, gather_all)
    f = Scatter(n, by, nz, bricks, *parts, scatter_all)
    factors = parts[0]

    def fetch(s, c):
        return pltpu.make_async_copy(views.at[s, c], seen_views.at[s, c], views_sem.at[s, c])

    for c in range(2):
        for s in range(slots):
            fetch(s, c).start()
    greet(n, nv, True)
    g.begin(0)
    g.zeros()
    s2[...] = jnp.zeros_like(s2)

    def bands(s, _):
        view = slot_views[s]
        build_bands(lambda a, k: psf[(view * 3 + a) * taps + k], dims, [m.at[s] for m in mats])
        return 0

    lax.fori_loop(0, slots, bands, 0)
    g.forward(0)
    g.begin(1)
    g.forward_sides(0)
    g.arrive(0)

    def run(c, s):
        brick = bricks[s]
        fetch(s, c).wait()

        def emit(rows, value):
            factors[s, c, rows, :] = value

        job(
            lambda y, count: blocks[c][pl.ds(brick * by + y, count)],
            lambda x: seen_views[s, c, x],
            background[slot_views[s]],
            dims,
            [m.at[s] for m in mats],
            s1,
            s2,
            emit,
        )

    def beside(c, s):
        if c == 0:

            @pl.when(s == 0)
            def _():
                g.forward(1)

            @pl.when(s == 1)
            def _():
                g.forward_sides(1)

        else:

            @pl.when(s == 0)
            def _():
                f.send(0)

    for c in range(2):

        def step(s, _):
            run(c, s)
            beside(c, s)
            return 0

        lax.fori_loop(0, slots, step, 0)
        if c == 0:
            g.arrive(1)
        f.begin(c)
    seen = crossing[0]
    for k in range(1, crossing.shape[0]):
        seen = seen + crossing[k]
    seen = seen.astype(F32)
    f.total(0)
    update(0, estimate, out, f.final, seen)
    f.send(1)
    for c in range(2):
        g.finish(c)
    f.total(1)
    update(1, estimate, out, f.final, seen)
    for c in range(2):
        f.finish(c)


def on_device(n, nv, estimate, view_data, psf, background, slot_brick, slot_view, intersection):
    channels, bx, by, nz = estimate.shape
    taps = psf.shape[2]
    halo = taps // 2
    dims = (taps, halo, bx, by, nz)
    slots, px, py = slot_brick.shape[2], bx + 2 * halo, by + 2 * halo
    est_wire = jnp.swapaxes(estimate.astype(BF16), 1, 2)
    wire = jnp.concatenate([est_wire[:, :, :HB], est_wire[:, :, bx - HB :]], axis=2)
    count = 2 * halo + by * n + ROWS - py
    return pl.pallas_call(
        functools.partial(kernel, n, nv, dims),
        out_shape=jax.ShapeDtypeStruct(estimate.shape, F32),
        in_specs=[VMEM, VMEM, pl.BlockSpec(memory_space=pl.ANY)] + [SMEM] * 5,
        out_specs=VMEM,
        scratch_shapes=[pltpu.VMEM((count, ROWS, nz), BF16)] * 2
        + [pltpu.VMEM((slots, channels, px, py, nz), BF16), pltpu.SemaphoreType.DMA((slots, channels))]
        + job_scratch(slots, nz)
        + scatter_scratch(n, slots, by, nz)
        + gather_sems(n)
        + scatter_sems(n),
        compiler_params=pltpu.CompilerParams(
            collective_id=0, has_side_effects=True, vmem_limit_bytes=60 * 1024 * 1024
        ),
    )(
        wire,
        estimate,
        view_data[0, 0],
        psf.reshape(-1),
        background,
        slot_brick[0, 0],
        slot_view[0, 0],
        intersection[0, 0],
    )


def solution(mesh):
    placed = (
        P(None, "view", "tile", None),
        P("view", "tile", None, None, None, None, None),
        P(),
        P(),
        P("view", "tile", None),
        P("view", "tile", None),
        P("view", "tile", None),
    )
    return jax.shard_map(
        functools.partial(on_device, mesh.shape["tile"], mesh.shape["view"]),
        mesh=mesh,
        in_specs=placed,
        out_specs=P(None, "view", "tile", None),
        check_vma=False,
    )
```

```python
import functools

import jax
import jax.numpy as jnp
from jax import lax
from jax.experimental import pallas as pl
from jax.experimental.pallas import tpu as pltpu
from jax.sharding import PartitionSpec as P

MESH = pl.DeviceIdType.MESH
F32 = jnp.float32
BF16 = jnp.bfloat16
ROWS = 64
HB = 16
UP = 32
PITCH1 = 72
PITCH2 = 40
GROUP = 8
VMEM = pl.BlockSpec(memory_space=pltpu.VMEM)
SMEM = pl.BlockSpec(memory_space=pltpu.SMEM)


def place(n):
    t, v = lax.axis_index("tile"), lax.axis_index("view")
    sib = t + 1 - 2 * lax.rem(t, 2)
    return t, v, sib


def same(t, step, n):
    return lax.rem(t + 2 * step + 2 * n, n)


def greet(n, nv, with_view):
    t, v, sib = place(n)
    barrier = pltpu.get_barrier_semaphore()

    def signal(tile, view):
        pl.semaphore_signal(barrier, inc=1, device_id=(tile, view), device_id_type=MESH)

    signal(sib, v)
    for k in range(1, n // 2):
        signal(same(t, k, n), v)
    peers = n // 2
    if with_view:

        @pl.when(v > 0)
        def _():
            signal(t, v - 1)

        @pl.when(v < nv - 1)
        def _():
            signal(t, v + 1)

        peers = peers + jnp.minimum(v, 1) + jnp.minimum(nv - 1 - v, 1)
    pl.semaphore_wait(barrier, peers)


class Gather:
    def __init__(self, n, nv, by, halo, wire, out, sems):
        self.n, self.nv, self.by, self.halo = n, nv, by, halo
        self.wire, self.out = wire, out
        self.sm, self.rm, self.sz, self.rz, self.ss, self.rs, self.loc = sems
        self.t, self.v, self.sib = place(n)

    def slab(self, c, b, part):
        start, size = ((HB, 2 * HB), (0, HB), (3 * HB, HB))[part]
        return self.out[c].at[pl.ds(self.halo + self.by * b, self.by), pl.ds(start, size), :]

    def copy(self, src, dst, s, r, dev):
        return pltpu.make_async_remote_copy(
            src_ref=src, dst_ref=dst, send_sem=s, recv_sem=r, device_id=dev, device_id_type=MESH
        )

    def main(self, c, k):
        return self.copy(
            self.wire.at[c],
            self.slab(c, self.t, 0),
            self.sm.at[c, k],
            self.rm.at[c, k],
            (same(self.t, k, self.n), self.v),
        )

    def to_sib(self, c, k, part):
        b = same(self.t, -k, self.n)
        src = self.wire.at[c] if (k == 0 and part == 0) else self.slab(c, b, part)
        return self.copy(
            src, self.slab(c, b, part), self.ss.at[c, k, part], self.rs.at[c, k, part], (self.sib, self.v)
        )

    def to_view(self, c, k, up):
        b = same(self.t, -k, self.n)
        first = HB if up else 0
        if k == 0:
            src = self.wire.at[c, :, pl.ds(first, HB), :]
        else:
            src = self.out[c].at[pl.ds(self.halo + self.by * b, self.by), pl.ds(HB + first, HB), :]
        side = 0 if up else 1
        return self.copy(
            src,
            self.slab(c, b, 1 if up else 2),
            self.sz.at[c, k, side],
            self.rz.at[c, k, side],
            (self.t, self.v + 1 if up else self.v - 1),
        )

    def local(self, c):
        return pltpu.make_async_copy(self.wire.at[c], self.slab(c, self.t, 0), self.loc.at[c])

    def views(self, c, k, act):
        @pl.when(self.v < self.nv - 1)
        def _():
            act(self.to_view(c, k, True))

        @pl.when(self.v > 0)
        def _():
            act(self.to_view(c, k, False))

    def zeros(self):
        count = self.out[0].shape[0]
        last = self.halo + self.by * self.n

        def fill(low, high, start, size):
            def body(i, _):
                for ref in self.out:
                    ref[pl.ds(i, 1), pl.ds(start, size), :] = jnp.zeros((1, size, ref.shape[2]), BF16)
                return 0

            lax.fori_loop(low, high, body, 0)

        fill(0, self.halo, 0, ROWS)
        fill(last, count, 0, ROWS)

        @pl.when(self.v == 0)
        def _():
            fill(self.halo, last, 0, HB)

        @pl.when(self.v == self.nv - 1)
        def _():
            fill(self.halo, last, 3 * HB, HB)

    def begin(self, c):
        for k in range(1, self.n // 2):
            self.main(c, k).start()
        self.views(c, 0, lambda d: d.start())
        self.to_sib(c, 0, 0).start()
        self.local(c).start()

    def forward(self, c):
        for k in range(1, self.n // 2):
            self.main(c, k).wait_recv()
            self.views(c, k, lambda d: d.start())
            self.to_sib(c, k, 0).start()

    def forward_sides(self, c):
        def side(k, part, when):
            @pl.when(when)
            def _():
                self.to_view(c, k, part == 1).wait_recv()
                self.to_sib(c, k, part).start()

        for k in range(self.n // 2):
            side(k, 1, self.v > 0)
            side(k, 2, self.v < self.nv - 1)

    def arrive(self, c):
        self.local(c).wait()
        for k in range(self.n // 2):
            self.to_sib(c, k, 0).wait_recv()

            @pl.when(self.v > 0)
            def _():
                self.to_sib(c, k, 1).wait_recv()

            @pl.when(self.v < self.nv - 1)
            def _():
                self.to_sib(c, k, 2).wait_recv()

    def finish(self, c):
        for k in range(self.n // 2):
            if k:
                self.main(c, k).wait_send()
            self.views(c, k, lambda d: d.wait_send())
            self.to_sib(c, k, 0).wait_send()

            @pl.when(self.v > 0)
            def _():
                self.to_sib(c, k, 1).wait_send()

            @pl.when(self.v < self.nv - 1)
            def _():
                self.to_sib(c, k, 2).wait_send()


def gather_sems(n):
    q = n // 2
    dma = pltpu.SemaphoreType.DMA
    return [dma((2, q)), dma((2, q)), dma((2, q, 2)), dma((2, q, 2)), dma((2, q, 3)), dma((2, q, 3)), dma((2,))]


def iota(shape, dim):
    return lax.broadcasted_iota(jnp.int32, shape, dim)


def split(x):
    hi = x.astype(BF16)
    return hi, (x - hi.astype(F32)).astype(BF16)


def band(tap, count, index, valid):
    index = jnp.where(valid, index, -1)
    total = jnp.zeros(index.shape, F32)
    for k in range(count):
        total = jnp.where(index == k, tap(k), total)
    return total


def build_bands(tap, dims, mats):
    fx, fy, cx, cy, fz, cz = mats
    taps, halo, bx, by, nz = dims
    px, py = bx + 2 * halo, by + 2 * halo

    def pieces(value, low):
        hi, lo = split(value)
        return jnp.where(low, lo.astype(F32), hi.astype(F32)).astype(BF16)

    p, col = iota((ROWS, 3 * ROWS), 0), iota((ROWS, 3 * ROWS), 1)
    low = (col >= ROWS) & (col < 2 * ROWS)
    r = jnp.where(col >= 2 * ROWS, col - 2 * ROWS, jnp.where(col >= ROWS, col - ROWS, col))
    gap = 2 * HB - (bx - HB) + HB
    x = jnp.where(r < 2 * HB, r - HB, r - gap + HB)
    fresh = (r < 2 * HB) | (x >= HB)
    q = x + halo
    valid = fresh & (q >= 0) & (q < px) & (p < px)
    fx[...] = pieces(band(lambda k: tap(0, k), taps, q - p + halo, valid), low)
    fy[...] = pieces(band(lambda k: tap(1, k), taps, r - p + halo, (r < py) & (p < py)), low)
    p, r, low = p[:UP], r[:UP], low[:UP]
    cx[...] = pieces(band(lambda k: tap(0, k), taps, p - r + 2 * halo, (r < px) & (p < bx)), low)
    cy[...] = pieces(band(lambda k: tap(1, k), taps, p - r + 2 * halo, (r < py) & (p < by)), low)
    z, w = iota((nz, nz), 0), iota((nz, nz), 1)
    hi, lo = split(band(lambda k: tap(2, k), taps, z - w + halo, w < nz))
    fz[...] = jnp.concatenate([hi, lo], axis=0)
    hi, lo = split(band(lambda k: tap(2, k), taps, w - z + halo, w < nz))
    back = jnp.concatenate([hi, lo], axis=1)
    cz[...] = jnp.concatenate([back, back], axis=0)


def stack(a, b):
    ah, al = split(a)
    bh, bl = split(b)
    hi = jnp.concatenate([ah, bh], axis=1)
    lo = jnp.concatenate([al, bl], axis=1)
    return jnp.concatenate([hi, hi, lo], axis=0)


def dot(a, b):
    return jnp.dot(a, b, preferred_element_type=F32)


def in_groups(count, size, body):
    full = count // size
    if full:

        def step(i, _):
            body(i * size, size)
            return 0

        lax.fori_loop(0, full, step, 0)
    if count % size:
        body(full * size, count % size)


def job(c, block, view, backdrop, dims, mats, s1, s2, vf, emit):
    fx, fy, cx, cy, fz, cz = mats
    taps, halo, bx, by, nz = dims
    px, py = bx + 2 * halo, by + 2 * halo

    def put(ref, line, pitch, size, value):
        ref[pl.ds(pl.multiple_of(line * pitch, 8), size), :] = value[:, :nz]
        ref[pl.ds(pl.multiple_of((line + 1) * pitch, 8), size), :] = value[:, nz:]

    def first(y, count):
        e = block(y, count).reshape(count * ROWS, nz)
        t = dot(jnp.concatenate([e, e], axis=1), fz[...])
        lines = [t[j * ROWS : (j + 1) * ROWS] for j in range(count)]
        done = [dot(fx[...], stack(lines[j], lines[j + 1])) for j in range(0, count, 2)]
        for j, u in enumerate(done):
            put(s1, y + 2 * j, PITCH1, ROWS, u)

    in_groups(ROWS, 16, first)

    def second(pair, count):
        done = []
        line = 2 * py
        vf[: count * 2 * line, :] = view(2 * pair, 2 * count).astype(F32)
        for j in range(count):
            x = 2 * (pair + j)
            a = s1[pl.ds(x, ROWS, PITCH1), :]
            b = s1[pl.ds(x + 1, ROWS, PITCH1), :]
            predicted = dot(fy[...], stack(a, b)) + backdrop
            va = vf[pl.ds(2 * j * line + c, ROWS, 2), :]
            vb = vf[pl.ds((2 * j + 1) * line + c, ROWS, 2), :]
            done.append((va / predicted[:, :nz], vb / predicted[:, nz:]))
        done = [dot(cy[...], stack(a, b)) for a, b in done]
        for j, f in enumerate(done):
            put(s2, 2 * (pair + j), PITCH2, UP, f)

    in_groups(px // 2, GROUP, second)

    def third(pair, count):
        done = []
        for j in range(count):
            y = 2 * (pair + j)
            a = s2[pl.ds(y, ROWS, PITCH2), :]
            b = s2[pl.ds(y + 1, ROWS, PITCH2), :]
            done.append(dot(cx[...], stack(a, b)))
        f = jnp.concatenate([v for f in done for v in (f[:, :nz], f[:, nz:])], axis=0)
        hi, lo = split(f)
        out = dot(jnp.concatenate([hi, lo], axis=1), cz[...])
        emit(pl.ds(pl.multiple_of(pair * 2 * UP, 8), count * 2 * UP), out[:, :nz] + out[:, nz:])

    in_groups(by // 2, 14, third)


def job_scratch(slots, py, nz):
    return [
        pltpu.VMEM((slots, ROWS, 3 * ROWS), BF16),
        pltpu.VMEM((slots, ROWS, 3 * ROWS), BF16),
        pltpu.VMEM((slots, UP, 3 * ROWS), BF16),
        pltpu.VMEM((slots, UP, 3 * ROWS), BF16),
        pltpu.VMEM((slots, 2 * nz, nz), BF16),
        pltpu.VMEM((slots, 2 * nz, 2 * nz), BF16),
        pltpu.VMEM((ROWS * PITCH1, nz), F32),
        pltpu.VMEM((ROWS * PITCH2, nz), F32),
        pltpu.VMEM((GROUP * 4 * py + 16, nz), F32),
    ]


class Scatter:
    def __init__(self, n, by, nz, bricks, factors, tx1, rx1, code, scale, code_in, scale_in, final, sems):
        self.n, self.nz, self.rows = n, nz, by * UP
        self.bricks, self.factors, self.tx1, self.rx1, self.final = bricks, factors, tx1, rx1, final
        self.code, self.scale, self.code_in, self.scale_in = code, scale, code_in, scale_in
        self.s1, self.r1, self.s2, self.r2 = sems
        self.t, self.v, self.sib = place(n)

    def own(self, c, o, rows):
        parts = [
            jnp.where(self.bricks[s] == o, self.factors[s, c, rows, :], 0.0)
            for s in range(self.factors.shape[0])
        ]
        return sum(parts[1:], parts[0])

    def loop(self, body, init=0):
        piece = 128

        def step(i, carry):
            return body(pl.ds(pl.multiple_of(i * piece, 16), piece), carry)

        return lax.fori_loop(0, self.rows // piece, step, init)

    def pair(self, c, j):
        return pltpu.make_async_remote_copy(
            src_ref=self.tx1.at[j, c],
            dst_ref=self.rx1.at[j, c],
            send_sem=self.s1.at[j, c],
            recv_sem=self.r1.at[j, c],
            device_id=(self.sib, self.v),
            device_id_type=MESH,
        )

    def chip(self, c, j, kind):
        src, dst = ((self.code, self.code_in), (self.scale, self.scale_in))[kind]
        return pltpu.make_async_remote_copy(
            src_ref=src.at[j, c],
            dst_ref=dst.at[j, c],
            send_sem=self.s2.at[j, c, kind],
            recv_sem=self.r2.at[j, c, kind],
            device_id=(same(self.t, j, self.n), self.v),
            device_id_type=MESH,
        )

    def begin(self, c):
        for j in list(range(1, self.n // 2)) + [0]:
            o = same(self.sib, j, self.n)

            def fill(rows, _):
                self.tx1[j, c, rows, :] = self.own(c, o, rows)
                return 0

            self.loop(fill)
            self.pair(c, j).start()

    def send(self, c):
        for j in range(1, self.n // 2):
            self.pair(c, j).wait_recv()
            o = same(self.t, j, self.n)

            def add(rows, top):
                value = self.own(c, o, rows) + self.rx1[j, c, rows, :]
                self.rx1[j, c, rows, :] = value
                return jnp.maximum(top, jnp.max(value.reshape(-1, 8, self.nz), axis=0))

            top = self.loop(add, jnp.zeros((8, self.nz), F32))
            top = jnp.max(top, axis=0, keepdims=True)
            top = jnp.where(top > 0.0, top, 1.0)
            self.scale[j, c] = jnp.broadcast_to(top, (8, self.nz))
            gain = 1.0 / top

            def pack(rows, _):
                level = jnp.minimum(self.rx1[j, c, rows, :] * gain * 65535.0, 65535.0)
                whole = jnp.round(level).astype(jnp.int32) - 32768
                self.code[j, c, rows, :] = whole.astype(jnp.int16)
                return 0

            self.loop(pack)
            self.chip(c, j, 0).start()
            self.chip(c, j, 1).start()

    def total(self, c):
        q = self.n // 2
        self.pair(c, 0).wait_recv()
        for j in range(1, q):
            self.chip(c, j, 0).wait_recv()
            self.chip(c, j, 1).wait_recv()

        def add(rows, _):
            value = self.own(c, self.t, rows) + self.rx1[0, c, rows, :]
            for j in range(1, q):
                level = self.code_in[j, c, rows, :].astype(jnp.int32).astype(F32) + 32768.0
                value = value + level * (self.scale_in[j, c, 0:1, :] * (1.0 / 65535.0))
            self.final[rows, :] = value
            return 0

        self.loop(add)

    def finish(self, c):
        for j in range(self.n // 2):
            self.pair(c, j).wait_send()
            if j:
                self.chip(c, j, 0).wait_send()
                self.chip(c, j, 1).wait_send()


def scatter_scratch(n, slots, by, nz):
    q, rows = n // 2, by * UP
    return [
        pltpu.VMEM((slots, 2, rows, nz), F32),
        pltpu.VMEM((q, 2, rows, nz), F32),
        pltpu.VMEM((q, 2, rows, nz), F32),
        pltpu.VMEM((q, 2, rows, nz), jnp.int16),
        pltpu.VMEM((q, 2, 8, nz), F32),
        pltpu.VMEM((q, 2, rows, nz), jnp.int16),
        pltpu.VMEM((q, 2, 8, nz), F32),
        pltpu.VMEM((rows, nz), F32),
    ]


def scatter_sems(n):
    q = n // 2
    dma = pltpu.SemaphoreType.DMA
    return [dma((q, 2)), dma((q, 2)), dma((q, 2, 2)), dma((q, 2, 2))]


def update(c, bx, by, estimate, out, total, seen):
    def body(u, _):
        where = pl.ds(u * 2 * by + c, by, 2)
        out[where, :] = estimate[where, :] * total[pl.ds(u, by, UP), :] / seen
        return 0

    lax.fori_loop(0, bx, body, 0)


def round_wire(c, bx, by, estimate, wire):
    def body(y, _):
        for start, first in ((0, 0), (HB, bx - HB)):
            rows = estimate[pl.ds(first * 2 * by + 2 * y + c, HB, 2 * by), :]
            wire[c, y, start : start + HB, :] = rows.astype(BF16)
        return 0

    lax.fori_loop(0, by, body, 0)


def kernel(n, nv, dims, estimate, views, psf, background, bricks, slot_views, crossing, out, *scratch):
    taps, halo, bx, by, nz = dims
    slots = views.shape[0]
    take = lambda count: [scratch.pop(0) for _ in range(count)]
    scratch = list(scratch)
    (wire,), blocks, (seen_views, views_sem) = take(1), take(2), take(2)
    mats, (s1, s2, vf), parts = take(6), take(3), take(8)
    gather_all, scatter_all = take(7), take(4)
    g = Gather(n, nv, by, halo, wire, blocks, gather_all)
    f = Scatter(n, by, nz, bricks, *parts, scatter_all)
    factors = parts[0]

    def fetch(s):
        return pltpu.make_async_copy(views.at[s], seen_views.at[s], views_sem.at[s])

    round_wire(0, bx, by, estimate, wire)
    greet(n, nv, True)
    g.begin(0)
    for s in range(slots):
        fetch(s).start()
    round_wire(1, bx, by, estimate, wire)
    g.zeros()
    s2[...] = jnp.zeros_like(s2)
    vf[...] = jnp.zeros_like(vf)

    def bands(s, _):
        view = slot_views[s]
        build_bands(lambda a, k: psf[view, a, k], dims, [m.at[s] for m in mats])
        return 0

    lax.fori_loop(0, slots, bands, 0)
    g.forward(0)
    g.begin(1)
    g.forward_sides(0)
    g.arrive(0)

    def run(c, s):
        brick = bricks[s]
        if c == 0:
            fetch(s).wait()

        def emit(rows, value):
            factors[s, c, rows, :] = value

        line = 2 * (by + 2 * halo)

        def view(x, count):
            return seen_views[s, pl.ds(pl.multiple_of(x * line, 16), count * line), :]

        job(
            c,
            lambda y, count: blocks[c][pl.ds(brick * by + y, count)],
            view,
            background[slot_views[s]],
            dims,
            [m.at[s] for m in mats],
            s1,
            s2,
            vf,
            emit,
        )

    def beside(c, s):
        if c == 0:

            @pl.when(s == 0)
            def _():
                g.forward(1)

            @pl.when(s == 1)
            def _():
                g.forward_sides(1)

        else:

            @pl.when(s == 0)
            def _():
                f.send(0)

    for c in range(2):

        def step(s, _):
            run(c, s)
            beside(c, s)
            return 0

        lax.fori_loop(0, slots, step, 0)
        if c == 0:
            g.arrive(1)
        f.begin(c)
    seen = crossing[0]
    for k in range(1, crossing.shape[0]):
        seen = seen + crossing[k]
    seen = seen.astype(F32)
    f.total(0)
    update(0, bx, by, estimate, out, f.final, seen)
    f.send(1)
    for c in range(2):
        g.finish(c)
    f.total(1)
    update(1, bx, by, estimate, out, f.final, seen)
    for c in range(2):
        f.finish(c)


def on_device(n, nv, estimate, view_data, psf, background, slot_brick, slot_view, intersection):
    channels, bx, by, nz = estimate.shape
    taps = psf.shape[2]
    halo = taps // 2
    dims = (taps, halo, bx, by, nz)
    slots, px, py = slot_brick.shape[2], bx + 2 * halo, by + 2 * halo
    cells = jnp.transpose(estimate, (1, 2, 0, 3)).reshape(bx * by * channels, nz)
    views = jnp.transpose(view_data[0, 0], (0, 2, 3, 1, 4)).reshape(slots, px * py * channels, nz)
    count = 2 * halo + by * n + ROWS - py
    updated = pl.pallas_call(
        functools.partial(kernel, n, nv, dims),
        out_shape=jax.ShapeDtypeStruct(cells.shape, F32),
        in_specs=[VMEM, pl.BlockSpec(memory_space=pl.ANY)] + [SMEM] * 5,
        out_specs=VMEM,
        scratch_shapes=[pltpu.VMEM((channels, by, UP, nz), BF16)]
        + [pltpu.VMEM((count, ROWS, nz), BF16)] * 2
        + [pltpu.VMEM((slots, px * py * channels, nz), BF16), pltpu.SemaphoreType.DMA((slots,))]
        + job_scratch(slots, py, nz)
        + scatter_scratch(n, slots, by, nz)
        + gather_sems(n)
        + scatter_sems(n),
        compiler_params=pltpu.CompilerParams(
            collective_id=0, has_side_effects=True, vmem_limit_bytes=60 * 1024 * 1024
        ),
    )(
        cells,
        views,
        psf,
        background,
        slot_brick[0, 0],
        slot_view[0, 0],
        intersection[0, 0],
    )
    return jnp.transpose(updated.reshape(bx, by, channels, nz), (2, 0, 1, 3))


def solution(mesh):
    placed = (
        P(None, "view", "tile", None),
        P("view", "tile", None, None, None, None, None),
        P(),
        P(),
        P("view", "tile", None),
        P("view", "tile", None),
        P("view", "tile", None),
    )
    return jax.shard_map(
        functools.partial(on_device, mesh.shape["tile"], mesh.shape["view"]),
        mesh=mesh,
        in_specs=placed,
        out_specs=P(None, "view", "tile", None),
        check_vma=False,
    )
```

```python
import functools

import jax
import jax.numpy as jnp
from jax import lax
from jax.experimental import pallas as pl
from jax.experimental.pallas import tpu as pltpu
from jax.sharding import PartitionSpec as P

MESH = pl.DeviceIdType.MESH
F32 = jnp.float32
BF16 = jnp.bfloat16
ROWS = 64
HB = 16
UP = 32
PITCH1 = 72
PITCH2 = 40
GROUP = 8
VMEM = pl.BlockSpec(memory_space=pltpu.VMEM)
SMEM = pl.BlockSpec(memory_space=pltpu.SMEM)


def place(n):
    t, v = lax.axis_index("tile"), lax.axis_index("view")
    sib = t + 1 - 2 * lax.rem(t, 2)
    return t, v, sib


def same(t, step, n):
    return lax.rem(t + 2 * step + 2 * n, n)


def greet(n, nv, with_view):
    t, v, sib = place(n)
    barrier = pltpu.get_barrier_semaphore()

    def signal(tile, view):
        pl.semaphore_signal(barrier, inc=1, device_id=(tile, view), device_id_type=MESH)

    signal(sib, v)
    for k in range(1, n // 2):
        signal(same(t, k, n), v)
    peers = n // 2
    if with_view:

        @pl.when(v > 0)
        def _():
            signal(t, v - 1)

        @pl.when(v < nv - 1)
        def _():
            signal(t, v + 1)

        peers = peers + jnp.minimum(v, 1) + jnp.minimum(nv - 1 - v, 1)
    pl.semaphore_wait(barrier, peers)


class Gather:
    def __init__(self, n, nv, by, halo, wire, out, sems):
        self.n, self.nv, self.by, self.halo = n, nv, by, halo
        self.wire, self.out = wire, out
        self.sm, self.rm, self.sz, self.rz, self.ss, self.rs, self.loc = sems
        self.t, self.v, self.sib = place(n)

    def slab(self, c, b, part):
        start, size = ((HB, 2 * HB), (0, HB), (3 * HB, HB))[part]
        return self.out[c].at[pl.ds(self.halo + self.by * b, self.by), pl.ds(start, size), :]

    def copy(self, src, dst, s, r, dev):
        return pltpu.make_async_remote_copy(
            src_ref=src, dst_ref=dst, send_sem=s, recv_sem=r, device_id=dev, device_id_type=MESH
        )

    def main(self, c, k):
        return self.copy(
            self.wire.at[c],
            self.slab(c, self.t, 0),
            self.sm.at[c, k],
            self.rm.at[c, k],
            (same(self.t, k, self.n), self.v),
        )

    def to_sib(self, c, k, part):
        b = same(self.t, -k, self.n)
        src = self.wire.at[c] if (k == 0 and part == 0) else self.slab(c, b, part)
        return self.copy(
            src, self.slab(c, b, part), self.ss.at[c, k, part], self.rs.at[c, k, part], (self.sib, self.v)
        )

    def to_view(self, c, k, up):
        b = same(self.t, -k, self.n)
        first = HB if up else 0
        if k == 0:
            src = self.wire.at[c, :, pl.ds(first, HB), :]
        else:
            src = self.out[c].at[pl.ds(self.halo + self.by * b, self.by), pl.ds(HB + first, HB), :]
        side = 0 if up else 1
        return self.copy(
            src,
            self.slab(c, b, 1 if up else 2),
            self.sz.at[c, k, side],
            self.rz.at[c, k, side],
            (self.t, self.v + 1 if up else self.v - 1),
        )

    def local(self, c):
        return pltpu.make_async_copy(self.wire.at[c], self.slab(c, self.t, 0), self.loc.at[c])

    def views(self, c, k, act):
        @pl.when(self.v < self.nv - 1)
        def _():
            act(self.to_view(c, k, True))

        @pl.when(self.v > 0)
        def _():
            act(self.to_view(c, k, False))

    def zeros(self):
        count = self.out[0].shape[0]
        last = self.halo + self.by * self.n

        def fill(low, high, start, size):
            def body(i, _):
                for ref in self.out:
                    ref[pl.ds(i, 1), pl.ds(start, size), :] = jnp.zeros((1, size, ref.shape[2]), BF16)
                return 0

            lax.fori_loop(low, high, body, 0)

        fill(0, self.halo, 0, ROWS)
        fill(last, count, 0, ROWS)

        @pl.when(self.v == 0)
        def _():
            fill(self.halo, last, 0, HB)

        @pl.when(self.v == self.nv - 1)
        def _():
            fill(self.halo, last, 3 * HB, HB)

    def begin(self, c):
        for k in range(1, self.n // 2):
            self.main(c, k).start()
        self.views(c, 0, lambda d: d.start())
        self.to_sib(c, 0, 0).start()
        self.local(c).start()

    def forward(self, c):
        for k in range(1, self.n // 2):
            self.main(c, k).wait_recv()
            self.views(c, k, lambda d: d.start())
            self.to_sib(c, k, 0).start()

    def forward_sides(self, c):
        def side(k, part, when):
            @pl.when(when)
            def _():
                self.to_view(c, k, part == 1).wait_recv()
                self.to_sib(c, k, part).start()

        for k in range(self.n // 2):
            side(k, 1, self.v > 0)
            side(k, 2, self.v < self.nv - 1)

    def arrive(self, c):
        self.local(c).wait()
        for k in range(self.n // 2):
            self.to_sib(c, k, 0).wait_recv()

            @pl.when(self.v > 0)
            def _():
                self.to_sib(c, k, 1).wait_recv()

            @pl.when(self.v < self.nv - 1)
            def _():
                self.to_sib(c, k, 2).wait_recv()

    def finish(self, c):
        for k in range(self.n // 2):
            if k:
                self.main(c, k).wait_send()
            self.views(c, k, lambda d: d.wait_send())
            self.to_sib(c, k, 0).wait_send()

            @pl.when(self.v > 0)
            def _():
                self.to_sib(c, k, 1).wait_send()

            @pl.when(self.v < self.nv - 1)
            def _():
                self.to_sib(c, k, 2).wait_send()


def gather_sems(n):
    q = n // 2
    dma = pltpu.SemaphoreType.DMA
    return [dma((2, q)), dma((2, q)), dma((2, q, 2)), dma((2, q, 2)), dma((2, q, 3)), dma((2, q, 3)), dma((2,))]


def iota(shape, dim):
    return lax.broadcasted_iota(jnp.int32, shape, dim)


def split(x):
    hi = x.astype(BF16)
    return hi, (x - hi.astype(F32)).astype(BF16)


def band(tap, count, index, valid):
    index = jnp.where(valid, index, -1)
    total = jnp.zeros(index.shape, F32)
    for k in range(count):
        total = jnp.where(index == k, tap(k), total)
    return total


def build_bands(tap, dims, mats):
    fx, fy, cx, cy, fz, cz = mats
    taps, halo, bx, by, nz = dims
    px, py = bx + 2 * halo, by + 2 * halo

    def keep(ref, value):
        ref[...] = jnp.concatenate(split(value), axis=0)

    p, col = iota((ROWS, 2 * ROWS), 0), iota((ROWS, 2 * ROWS), 1)
    r = jnp.where(col >= ROWS, col - ROWS, col)
    gap = 2 * HB - (bx - HB) + HB
    x = jnp.where(r < 2 * HB, r - HB, r - gap + HB)
    fresh = (r < 2 * HB) | (x >= HB)
    q = x + halo
    valid = fresh & (q >= 0) & (q < px) & (p < px)
    keep(fx, band(lambda k: tap(0, k), taps, q - p + halo, valid)[:, :ROWS])
    keep(fy, band(lambda k: tap(1, k), taps, r - p + halo, (r < py) & (p < py)))
    p, r = p[:UP], r[:UP]
    keep(cx, band(lambda k: tap(0, k), taps, p - r + 2 * halo, (r < px) & (p < bx)))
    keep(cy, band(lambda k: tap(1, k), taps, p - r + 2 * halo, (r < py) & (p < by)))
    z, w = iota((nz, nz), 0), iota((nz, nz), 1)
    for ref, offset in ((fz, z - w), (cz, w - z)):
        both = jnp.concatenate(split(band(lambda k: tap(2, k), taps, offset + halo, w < nz)), axis=1)
        ref[...] = jnp.concatenate([both, both], axis=0)


def dot(a, b):
    return jnp.dot(a, b, preferred_element_type=F32)


def along(mat, a, b):
    both = jnp.concatenate([a, b], axis=1)
    if both.dtype != BF16:
        both = jnp.concatenate(split(both), axis=0)
    out = dot(mat[...], both)
    half = out.shape[0] // 2
    return out[:half] + out[half:]


def along_last(x, mat):
    out = dot(jnp.concatenate(split(x), axis=1), mat[...])
    half = out.shape[1] // 2
    return out[:, :half] + out[:, half:]


def apart(pairs, nz):
    return jnp.concatenate([v for f in pairs for v in (f[:, :nz], f[:, nz:])], axis=0)


def in_groups(count, size, body):
    full = count // size
    if full:

        def step(i, _):
            body(i * size, size)
            return 0

        lax.fori_loop(0, full, step, 0)
    if count % size:
        body(full * size, count % size)


def job(c, block, view, backdrop, dims, mats, s1, s2, vf, emit):
    fx, fy, cx, cy, fz, cz = mats
    taps, halo, bx, by, nz = dims
    px, py = bx + 2 * halo, by + 2 * halo

    def put(ref, line, pitch, size, value):
        ref[pl.ds(pl.multiple_of(line * pitch, 8), size), :] = value[:, :nz]
        ref[pl.ds(pl.multiple_of((line + 1) * pitch, 8), size), :] = value[:, nz:]

    def first(y, count):
        e = block(y, count)
        u = apart([along(fx, e[j], e[j + 1]) for j in range(0, count, 2)], nz)
        t = along_last(u, fz)
        for j in range(count):
            s1[pl.ds(pl.multiple_of((y + j) * PITCH1, 8), ROWS), :] = t[j * ROWS : (j + 1) * ROWS]

    in_groups(ROWS, 16, first)

    def second(pair, count):
        done = []
        line = 2 * py
        vf[: count * 2 * line, :] = view(2 * pair, 2 * count).astype(F32)
        for j in range(count):
            x = 2 * (pair + j)
            a = s1[pl.ds(x, ROWS, PITCH1), :]
            b = s1[pl.ds(x + 1, ROWS, PITCH1), :]
            predicted = along(fy, a, b) + backdrop
            va = vf[pl.ds(2 * j * line + c, ROWS, 2), :]
            vb = vf[pl.ds((2 * j + 1) * line + c, ROWS, 2), :]
            done.append((va / predicted[:, :nz], vb / predicted[:, nz:]))
        done = [along(cy, a, b) for a, b in done]
        for j, f in enumerate(done):
            put(s2, 2 * (pair + j), PITCH2, UP, f)

    in_groups(px // 2, GROUP, second)

    def third(pair, count):
        done = []
        for j in range(count):
            y = 2 * (pair + j)
            a = s2[pl.ds(y, ROWS, PITCH2), :]
            b = s2[pl.ds(y + 1, ROWS, PITCH2), :]
            done.append(along(cx, a, b))
        out = along_last(apart(done, nz), cz)
        emit(pl.ds(pl.multiple_of(pair * 2 * UP, 8), count * 2 * UP), out)

    in_groups(by // 2, 14, third)


def job_scratch(slots, py, nz):
    return [
        pltpu.VMEM((slots, 2 * ROWS, ROWS), BF16),
        pltpu.VMEM((slots, 2 * ROWS, 2 * ROWS), BF16),
        pltpu.VMEM((slots, 2 * UP, 2 * ROWS), BF16),
        pltpu.VMEM((slots, 2 * UP, 2 * ROWS), BF16),
        pltpu.VMEM((slots, 2 * nz, 2 * nz), BF16),
        pltpu.VMEM((slots, 2 * nz, 2 * nz), BF16),
        pltpu.VMEM((ROWS * PITCH1, nz), F32),
        pltpu.VMEM((ROWS * PITCH2, nz), F32),
        pltpu.VMEM((GROUP * 4 * py + 16, nz), F32),
    ]


class Scatter:
    def __init__(self, n, by, nz, bricks, factors, tx1, rx1, code, scale, code_in, scale_in, final, sems):
        self.n, self.nz, self.rows = n, nz, by * UP
        self.bricks, self.factors, self.tx1, self.rx1, self.final = bricks, factors, tx1, rx1, final
        self.code, self.scale, self.code_in, self.scale_in = code, scale, code_in, scale_in
        self.s1, self.r1, self.s2, self.r2 = sems
        self.t, self.v, self.sib = place(n)

    def own(self, c, o, rows):
        parts = [
            jnp.where(self.bricks[s] == o, self.factors[s, c, rows, :], 0.0)
            for s in range(self.factors.shape[0])
        ]
        return sum(parts[1:], parts[0])

    def loop(self, body, init=0):
        piece = 128

        def step(i, carry):
            return body(pl.ds(pl.multiple_of(i * piece, 16), piece), carry)

        return lax.fori_loop(0, self.rows // piece, step, init)

    def pair(self, c, j):
        return pltpu.make_async_remote_copy(
            src_ref=self.tx1.at[j, c],
            dst_ref=self.rx1.at[j, c],
            send_sem=self.s1.at[j, c],
            recv_sem=self.r1.at[j, c],
            device_id=(self.sib, self.v),
            device_id_type=MESH,
        )

    def chip(self, c, j, kind):
        src, dst = ((self.code, self.code_in), (self.scale, self.scale_in))[kind]
        return pltpu.make_async_remote_copy(
            src_ref=src.at[j, c],
            dst_ref=dst.at[j, c],
            send_sem=self.s2.at[j, c, kind],
            recv_sem=self.r2.at[j, c, kind],
            device_id=(same(self.t, j, self.n), self.v),
            device_id_type=MESH,
        )

    def begin(self, c):
        for j in list(range(1, self.n // 2)) + [0]:
            o = same(self.sib, j, self.n)

            def fill(rows, _):
                self.tx1[j, c, rows, :] = self.own(c, o, rows)
                return 0

            self.loop(fill)
            self.pair(c, j).start()

    def send(self, c):
        for j in range(1, self.n // 2):
            self.pair(c, j).wait_recv()
            o = same(self.t, j, self.n)

            def add(rows, top):
                value = self.own(c, o, rows) + self.rx1[j, c, rows, :]
                self.rx1[j, c, rows, :] = value
                return jnp.maximum(top, jnp.max(value.reshape(-1, 8, self.nz), axis=0))

            top = self.loop(add, jnp.zeros((8, self.nz), F32))
            top = jnp.max(top, axis=0, keepdims=True)
            top = jnp.where(top > 0.0, top, 1.0)
            self.scale[j, c] = jnp.broadcast_to(top, (8, self.nz))
            gain = 1.0 / top

            def pack(rows, _):
                level = jnp.minimum(self.rx1[j, c, rows, :] * gain * 65535.0, 65535.0)
                whole = jnp.round(level).astype(jnp.int32) - 32768
                self.code[j, c, rows, :] = whole.astype(jnp.int16)
                return 0

            self.loop(pack)
            self.chip(c, j, 0).start()
            self.chip(c, j, 1).start()

    def total(self, c):
        q = self.n // 2
        self.pair(c, 0).wait_recv()
        for j in range(1, q):
            self.chip(c, j, 0).wait_recv()
            self.chip(c, j, 1).wait_recv()

        def add(rows, _):
            value = self.own(c, self.t, rows) + self.rx1[0, c, rows, :]
            for j in range(1, q):
                level = self.code_in[j, c, rows, :].astype(jnp.int32).astype(F32) + 32768.0
                value = value + level * (self.scale_in[j, c, 0:1, :] * (1.0 / 65535.0))
            self.final[rows, :] = value
            return 0

        self.loop(add)

    def finish(self, c):
        for j in range(self.n // 2):
            self.pair(c, j).wait_send()
            if j:
                self.chip(c, j, 0).wait_send()
                self.chip(c, j, 1).wait_send()


def scatter_scratch(n, slots, by, nz):
    q, rows = n // 2, by * UP
    return [
        pltpu.VMEM((slots, 2, rows, nz), F32),
        pltpu.VMEM((q, 2, rows, nz), F32),
        pltpu.VMEM((q, 2, rows, nz), F32),
        pltpu.VMEM((q, 2, rows, nz), jnp.int16),
        pltpu.VMEM((q, 2, 8, nz), F32),
        pltpu.VMEM((q, 2, rows, nz), jnp.int16),
        pltpu.VMEM((q, 2, 8, nz), F32),
        pltpu.VMEM((rows, nz), F32),
    ]


def scatter_sems(n):
    q = n // 2
    dma = pltpu.SemaphoreType.DMA
    return [dma((q, 2)), dma((q, 2)), dma((q, 2, 2)), dma((q, 2, 2))]


def update(c, bx, by, estimate, out, total, seen):
    def body(u, _):
        where = pl.ds(u * 2 * by + c, by, 2)
        out[where, :] = estimate[where, :] * total[pl.ds(u, by, UP), :] / seen
        return 0

    lax.fori_loop(0, bx, body, 0)


def round_wire(c, bx, by, estimate, wire):
    def body(y, _):
        for start, first in ((0, 0), (HB, bx - HB)):
            rows = estimate[pl.ds(first * 2 * by + 2 * y + c, HB, 2 * by), :]
            wire[c, y, start : start + HB, :] = rows.astype(BF16)
        return 0

    lax.fori_loop(0, by, body, 0)


def kernel(n, nv, dims, estimate, views, psf, background, bricks, slot_views, crossing, out, *scratch):
    taps, halo, bx, by, nz = dims
    slots = views.shape[0]
    take = lambda count: [scratch.pop(0) for _ in range(count)]
    scratch = list(scratch)
    (wire,), blocks, (seen_views, views_sem) = take(1), take(2), take(2)
    mats, (s1, s2, vf), parts = take(6), take(3), take(8)
    gather_all, scatter_all = take(7), take(4)
    g = Gather(n, nv, by, halo, wire, blocks, gather_all)
    f = Scatter(n, by, nz, bricks, *parts, scatter_all)
    factors = parts[0]

    def fetch(s):
        return pltpu.make_async_copy(views.at[s], seen_views.at[s], views_sem.at[s])

    round_wire(0, bx, by, estimate, wire)
    greet(n, nv, True)
    g.begin(0)
    for s in range(slots):
        fetch(s).start()
    round_wire(1, bx, by, estimate, wire)
    g.zeros()
    s2[...] = jnp.zeros_like(s2)
    vf[...] = jnp.zeros_like(vf)

    def bands(s, _):
        view = slot_views[s]
        build_bands(lambda a, k: psf[view, a, k], dims, [m.at[s] for m in mats])
        return 0

    lax.fori_loop(0, slots, bands, 0)
    g.forward(0)
    g.begin(1)
    g.forward_sides(0)
    g.arrive(0)

    def run(c, s):
        brick = bricks[s]
        if c == 0:
            fetch(s).wait()

        def emit(rows, value):
            factors[s, c, rows, :] = value

        line = 2 * (by + 2 * halo)

        def view(x, count):
            return seen_views[s, pl.ds(pl.multiple_of(x * line, 16), count * line), :]

        job(
            c,
            lambda y, count: blocks[c][pl.ds(brick * by + y, count)],
            view,
            background[slot_views[s]],
            dims,
            [m.at[s] for m in mats],
            s1,
            s2,
            vf,
            emit,
        )

    def beside(c, s):
        if c == 0:

            @pl.when(s == 0)
            def _():
                g.forward(1)

            @pl.when(s == 1)
            def _():
                g.forward_sides(1)

        else:

            @pl.when(s == 0)
            def _():
                f.send(0)

    for c in range(2):

        def step(s, _):
            run(c, s)
            beside(c, s)
            return 0

        lax.fori_loop(0, slots, step, 0)
        if c == 0:
            g.arrive(1)
        f.begin(c)
    seen = crossing[0]
    for k in range(1, crossing.shape[0]):
        seen = seen + crossing[k]
    seen = seen.astype(F32)
    f.total(0)
    update(0, bx, by, estimate, out, f.final, seen)
    f.send(1)
    for c in range(2):
        g.finish(c)
    f.total(1)
    update(1, bx, by, estimate, out, f.final, seen)
    for c in range(2):
        f.finish(c)


def on_device(n, nv, estimate, view_data, psf, background, slot_brick, slot_view, intersection):
    channels, bx, by, nz = estimate.shape
    taps = psf.shape[2]
    halo = taps // 2
    dims = (taps, halo, bx, by, nz)
    slots, px, py = slot_brick.shape[2], bx + 2 * halo, by + 2 * halo
    cells = jnp.transpose(estimate, (1, 2, 0, 3)).reshape(bx * by * channels, nz)
    views = jnp.transpose(view_data[0, 0], (0, 2, 3, 1, 4)).reshape(slots, px * py * channels, nz)
    count = 2 * halo + by * n + ROWS - py
    updated = pl.pallas_call(
        functools.partial(kernel, n, nv, dims),
        out_shape=jax.ShapeDtypeStruct(cells.shape, F32),
        in_specs=[VMEM, pl.BlockSpec(memory_space=pl.ANY)] + [SMEM] * 5,
        out_specs=VMEM,
        scratch_shapes=[pltpu.VMEM((channels, by, UP, nz), BF16)]
        + [pltpu.VMEM((count, ROWS, nz), BF16)] * 2
        + [pltpu.VMEM((slots, px * py * channels, nz), BF16), pltpu.SemaphoreType.DMA((slots,))]
        + job_scratch(slots, py, nz)
        + scatter_scratch(n, slots, by, nz)
        + gather_sems(n)
        + scatter_sems(n),
        compiler_params=pltpu.CompilerParams(
            collective_id=0, has_side_effects=True, vmem_limit_bytes=60 * 1024 * 1024
        ),
    )(
        cells,
        views,
        psf,
        background,
        slot_brick[0, 0],
        slot_view[0, 0],
        intersection[0, 0],
    )
    return jnp.transpose(updated.reshape(bx, by, channels, nz), (2, 0, 1, 3))


def solution(mesh):
    placed = (
        P(None, "view", "tile", None),
        P("view", "tile", None, None, None, None, None),
        P(),
        P(),
        P("view", "tile", None),
        P("view", "tile", None),
        P("view", "tile", None),
    )
    return jax.shard_map(
        functools.partial(on_device, mesh.shape["tile"], mesh.shape["view"]),
        mesh=mesh,
        in_specs=placed,
        out_specs=P(None, "view", "tile", None),
        check_vma=False,
    )
```

```python
import functools

import jax
import jax.numpy as jnp
from jax import lax
from jax.experimental import pallas as pl
from jax.experimental.pallas import tpu as pltpu
from jax.sharding import PartitionSpec as P

MESH = pl.DeviceIdType.MESH
F32 = jnp.float32
BF16 = jnp.bfloat16
ROWS = 64
HB = 16
UP = 32
PITCH1 = 72
PITCH2 = 40
GROUP = 8
VMEM = pl.BlockSpec(memory_space=pltpu.VMEM)
SMEM = pl.BlockSpec(memory_space=pltpu.SMEM)


def place(n):
    t, v = lax.axis_index("tile"), lax.axis_index("view")
    sib = t + 1 - 2 * lax.rem(t, 2)
    return t, v, sib


def same(t, step, n):
    return lax.rem(t + 2 * step + 2 * n, n)


def greet(n, nv, with_view):
    t, v, sib = place(n)
    barrier = pltpu.get_barrier_semaphore()

    def signal(tile, view):
        pl.semaphore_signal(barrier, inc=1, device_id=(tile, view), device_id_type=MESH)

    signal(sib, v)
    for k in range(1, n // 2):
        signal(same(t, k, n), v)
    peers = n // 2
    if with_view:

        @pl.when(v > 0)
        def _():
            signal(t, v - 1)

        @pl.when(v < nv - 1)
        def _():
            signal(t, v + 1)

        peers = peers + jnp.minimum(v, 1) + jnp.minimum(nv - 1 - v, 1)
    pl.semaphore_wait(barrier, peers)


class Gather:
    def __init__(self, n, nv, by, halo, wire, out, sems):
        self.n, self.nv, self.by, self.halo = n, nv, by, halo
        self.wire, self.out = wire, out
        self.sm, self.rm, self.sz, self.rz, self.ss, self.rs, self.loc = sems
        self.t, self.v, self.sib = place(n)

    def slab(self, c, b, part):
        start, size = ((HB, 2 * HB), (0, HB), (3 * HB, HB))[part]
        return self.out[c].at[pl.ds(self.halo + self.by * b, self.by), pl.ds(start, size), :]

    def copy(self, src, dst, s, r, dev):
        return pltpu.make_async_remote_copy(
            src_ref=src, dst_ref=dst, send_sem=s, recv_sem=r, device_id=dev, device_id_type=MESH
        )

    def main(self, c, k):
        return self.copy(
            self.wire.at[c],
            self.slab(c, self.t, 0),
            self.sm.at[c, k],
            self.rm.at[c, k],
            (same(self.t, k, self.n), self.v),
        )

    def to_sib(self, c, k, part):
        b = same(self.t, -k, self.n)
        src = self.wire.at[c] if (k == 0 and part == 0) else self.slab(c, b, part)
        return self.copy(
            src, self.slab(c, b, part), self.ss.at[c, k, part], self.rs.at[c, k, part], (self.sib, self.v)
        )

    def to_view(self, c, k, up):
        b = same(self.t, -k, self.n)
        first = HB if up else 0
        if k == 0:
            src = self.wire.at[c, :, pl.ds(first, HB), :]
        else:
            src = self.out[c].at[pl.ds(self.halo + self.by * b, self.by), pl.ds(HB + first, HB), :]
        side = 0 if up else 1
        return self.copy(
            src,
            self.slab(c, b, 1 if up else 2),
            self.sz.at[c, k, side],
            self.rz.at[c, k, side],
            (self.t, self.v + 1 if up else self.v - 1),
        )

    def local(self, c):
        return pltpu.make_async_copy(self.wire.at[c], self.slab(c, self.t, 0), self.loc.at[c])

    def views(self, c, k, act):
        @pl.when(self.v < self.nv - 1)
        def _():
            act(self.to_view(c, k, True))

        @pl.when(self.v > 0)
        def _():
            act(self.to_view(c, k, False))

    def zeros(self):
        count = self.out[0].shape[0]
        last = self.halo + self.by * self.n

        def fill(low, high, start, size):
            def body(i, _):
                for ref in self.out:
                    ref[pl.ds(i, 1), pl.ds(start, size), :] = jnp.zeros((1, size, ref.shape[2]), BF16)
                return 0

            lax.fori_loop(low, high, body, 0)

        fill(0, self.halo, 0, ROWS)
        fill(last, count, 0, ROWS)

        @pl.when(self.v == 0)
        def _():
            fill(self.halo, last, 0, HB)

        @pl.when(self.v == self.nv - 1)
        def _():
            fill(self.halo, last, 3 * HB, HB)

    def begin(self, c):
        for k in range(1, self.n // 2):
            self.main(c, k).start()
        self.views(c, 0, lambda d: d.start())
        self.to_sib(c, 0, 0).start()
        self.local(c).start()

    def forward(self, c):
        for k in range(1, self.n // 2):
            self.main(c, k).wait_recv()
            self.views(c, k, lambda d: d.start())
            self.to_sib(c, k, 0).start()

    def forward_sides(self, c):
        def side(k, part, when):
            @pl.when(when)
            def _():
                self.to_view(c, k, part == 1).wait_recv()
                self.to_sib(c, k, part).start()

        for k in range(self.n // 2):
            side(k, 1, self.v > 0)
            side(k, 2, self.v < self.nv - 1)

    def arrive(self, c):
        self.local(c).wait()
        for k in range(self.n // 2):
            self.to_sib(c, k, 0).wait_recv()

            @pl.when(self.v > 0)
            def _():
                self.to_sib(c, k, 1).wait_recv()

            @pl.when(self.v < self.nv - 1)
            def _():
                self.to_sib(c, k, 2).wait_recv()

    def finish(self, c):
        for k in range(self.n // 2):
            if k:
                self.main(c, k).wait_send()
            self.views(c, k, lambda d: d.wait_send())
            self.to_sib(c, k, 0).wait_send()

            @pl.when(self.v > 0)
            def _():
                self.to_sib(c, k, 1).wait_send()

            @pl.when(self.v < self.nv - 1)
            def _():
                self.to_sib(c, k, 2).wait_send()


def gather_sems(n):
    q = n // 2
    dma = pltpu.SemaphoreType.DMA
    return [dma((2, q)), dma((2, q)), dma((2, q, 2)), dma((2, q, 2)), dma((2, q, 3)), dma((2, q, 3)), dma((2,))]


def iota(shape, dim):
    return lax.broadcasted_iota(jnp.int32, shape, dim)


def split(x):
    hi = x.astype(BF16)
    return hi, (x - hi.astype(F32)).astype(BF16)


def band(tap, count, index, valid):
    index = jnp.where(valid, index, -1)
    total = jnp.zeros(index.shape, F32)
    for k in range(count):
        total = jnp.where(index == k, tap(k), total)
    return total


def build_bands(tap, dims, mats):
    fx, fy, cx, cy, fz, cz = mats
    taps, halo, bx, by, nz = dims
    px, py = bx + 2 * halo, by + 2 * halo

    def keep(ref, value):
        ref[...] = jnp.concatenate(split(value), axis=0)

    p, col = iota((ROWS, 2 * ROWS), 0), iota((ROWS, 2 * ROWS), 1)
    r = jnp.where(col >= ROWS, col - ROWS, col)
    gap = 2 * HB - (bx - HB) + HB
    x = jnp.where(r < 2 * HB, r - HB, r - gap + HB)
    fresh = (r < 2 * HB) | (x >= HB)
    q = x + halo
    valid = fresh & (q >= 0) & (q < px) & (p < px)
    keep(fx, band(lambda k: tap(0, k), taps, q - p + halo, valid)[:, :ROWS])
    keep(fy, band(lambda k: tap(1, k), taps, r - p + halo, (r < py) & (p < py)))
    p, r = p[:UP], r[:UP]
    keep(cx, band(lambda k: tap(0, k), taps, p - r + 2 * halo, (r < px) & (p < bx)))
    keep(cy, band(lambda k: tap(1, k), taps, p - r + 2 * halo, (r < py) & (p < by)))
    z, w = iota((nz, nz), 0), iota((nz, nz), 1)
    for ref, offset in ((fz, z - w), (cz, w - z)):
        both = jnp.concatenate(split(band(lambda k: tap(2, k), taps, offset + halo, w < nz)), axis=1)
        ref[...] = jnp.concatenate([both, both], axis=0)


def dot(a, b):
    return jnp.dot(a, b, preferred_element_type=F32)


def along(mat, a, b):
    both = jnp.concatenate([a, b], axis=1)
    if both.dtype != BF16:
        both = jnp.concatenate(split(both), axis=0)
    out = dot(mat[...], both)
    half = out.shape[0] // 2
    return out[:half] + out[half:]


def along_last(x, mat):
    out = dot(jnp.concatenate(split(x), axis=1), mat[...])
    half = out.shape[1] // 2
    return out[:, :half] + out[:, half:]


def apart(pairs, nz):
    return jnp.concatenate([v for f in pairs for v in (f[:, :nz], f[:, nz:])], axis=0)


def in_groups(count, size, body):
    full = count // size
    if full:

        def step(i, _):
            body(i * size, size)
            return 0

        lax.fori_loop(0, full, step, 0)
    if count % size:
        body(full * size, count % size)


def skewed(items, stages):
    items, held = list(items), {}
    for step in range(len(items) + len(stages) - 1):
        for depth, stage in enumerate(stages):
            i = step - depth
            if 0 <= i < len(items):
                held[i] = stage(items[i], held[i]) if depth else stage(items[i])


def job(c, block, view, backdrop, dims, mats, s1, s2, vf, emit):
    fx, fy, cx, cy, fz, cz = mats
    taps, halo, bx, by, nz = dims
    px, py = bx + 2 * halo, by + 2 * halo

    def put(ref, line, pitch, size, value):
        ref[pl.ds(pl.multiple_of(line * pitch, 8), size), :] = value[:, :nz]
        ref[pl.ds(pl.multiple_of((line + 1) * pitch, 8), size), :] = value[:, nz:]

    def first(y, count):
        e = block(y, count)
        part = 4

        def ahead(k):
            return apart([along(fx, e[j], e[j + 1]) for j in range(k, k + part, 2)], nz)

        def after(k, u):
            t = along_last(u, fz)
            for j in range(part):
                s1[pl.ds(pl.multiple_of((y + k + j) * PITCH1, 8), ROWS), :] = t[j * ROWS : (j + 1) * ROWS]

        skewed(range(0, count, part), [ahead, after])

    in_groups(ROWS, 16, first)

    def second(pair, count):
        line = 2 * py
        vf[: count * 2 * line, :] = view(2 * pair, 2 * count).astype(F32)

        def forward(j):
            x = 2 * (pair + j)
            return along(fy, s1[pl.ds(x, ROWS, PITCH1), :], s1[pl.ds(x + 1, ROWS, PITCH1), :])

        def ratio(j, blurred):
            predicted = blurred + backdrop
            va = vf[pl.ds(2 * j * line + c, ROWS, 2), :]
            vb = vf[pl.ds((2 * j + 1) * line + c, ROWS, 2), :]
            return va / predicted[:, :nz], vb / predicted[:, nz:]

        def back(j, lines):
            put(s2, 2 * (pair + j), PITCH2, UP, along(cy, *lines))

        skewed(range(count), [forward, ratio, back])

    in_groups(px // 2, GROUP, second)

    def third(pair, count):
        part = 2

        def ahead(k):
            lines = []
            for j in range(k, min(k + part, count)):
                y = 2 * (pair + j)
                lines.append(along(cx, s2[pl.ds(y, ROWS, PITCH2), :], s2[pl.ds(y + 1, ROWS, PITCH2), :]))
            return apart(lines, nz)

        def after(k, f):
            emit(pl.ds(pl.multiple_of((pair + k) * 2 * UP, 8), f.shape[0]), along_last(f, cz))

        skewed(range(0, count, part), [ahead, after])

    in_groups(by // 2, 14, third)


def job_scratch(slots, py, nz):
    return [
        pltpu.VMEM((slots, 2 * ROWS, ROWS), BF16),
        pltpu.VMEM((slots, 2 * ROWS, 2 * ROWS), BF16),
        pltpu.VMEM((slots, 2 * UP, 2 * ROWS), BF16),
        pltpu.VMEM((slots, 2 * UP, 2 * ROWS), BF16),
        pltpu.VMEM((slots, 2 * nz, 2 * nz), BF16),
        pltpu.VMEM((slots, 2 * nz, 2 * nz), BF16),
        pltpu.VMEM((ROWS * PITCH1, nz), F32),
        pltpu.VMEM((ROWS * PITCH2, nz), F32),
        pltpu.VMEM((GROUP * 4 * py + 16, nz), F32),
    ]


class Scatter:
    def __init__(self, n, by, nz, bricks, factors, tx1, rx1, code, scale, code_in, scale_in, final, sems):
        self.n, self.nz, self.rows = n, nz, by * UP
        self.bricks, self.factors, self.tx1, self.rx1, self.final = bricks, factors, tx1, rx1, final
        self.code, self.scale, self.code_in, self.scale_in = code, scale, code_in, scale_in
        self.s1, self.r1, self.s2, self.r2 = sems
        self.t, self.v, self.sib = place(n)

    def own(self, c, o, rows):
        parts = [
            jnp.where(self.bricks[s] == o, self.factors[s, c, rows, :], 0.0)
            for s in range(self.factors.shape[0])
        ]
        return sum(parts[1:], parts[0])

    def loop(self, body, init=0):
        piece = 128

        def step(i, carry):
            return body(pl.ds(pl.multiple_of(i * piece, 16), piece), carry)

        return lax.fori_loop(0, self.rows // piece, step, init)

    def pair(self, c, j):
        return pltpu.make_async_remote_copy(
            src_ref=self.tx1.at[j, c],
            dst_ref=self.rx1.at[j, c],
            send_sem=self.s1.at[j, c],
            recv_sem=self.r1.at[j, c],
            device_id=(self.sib, self.v),
            device_id_type=MESH,
        )

    def chip(self, c, j, kind):
        src, dst = ((self.code, self.code_in), (self.scale, self.scale_in))[kind]
        return pltpu.make_async_remote_copy(
            src_ref=src.at[j, c],
            dst_ref=dst.at[j, c],
            send_sem=self.s2.at[j, c, kind],
            recv_sem=self.r2.at[j, c, kind],
            device_id=(same(self.t, j, self.n), self.v),
            device_id_type=MESH,
        )

    def begin(self, c):
        for j in list(range(1, self.n // 2)) + [0]:
            o = same(self.sib, j, self.n)

            def fill(rows, _):
                self.tx1[j, c, rows, :] = self.own(c, o, rows)
                return 0

            self.loop(fill)
            self.pair(c, j).start()

    def send(self, c):
        for j in range(1, self.n // 2):
            self.pair(c, j).wait_recv()
            o = same(self.t, j, self.n)

            def add(rows, top):
                value = self.own(c, o, rows) + self.rx1[j, c, rows, :]
                self.rx1[j, c, rows, :] = value
                return jnp.maximum(top, jnp.max(value.reshape(-1, 8, self.nz), axis=0))

            top = self.loop(add, jnp.zeros((8, self.nz), F32))
            top = jnp.max(top, axis=0, keepdims=True)
            top = jnp.where(top > 0.0, top, 1.0)
            self.scale[j, c] = jnp.broadcast_to(top, (8, self.nz))
            gain = 1.0 / top

            def pack(rows, _):
                level = jnp.minimum(self.rx1[j, c, rows, :] * gain * 65535.0, 65535.0)
                whole = jnp.round(level).astype(jnp.int32) - 32768
                self.code[j, c, rows, :] = whole.astype(jnp.int16)
                return 0

            self.loop(pack)
            self.chip(c, j, 0).start()
            self.chip(c, j, 1).start()

    def total(self, c):
        q = self.n // 2
        self.pair(c, 0).wait_recv()
        for j in range(1, q):
            self.chip(c, j, 0).wait_recv()
            self.chip(c, j, 1).wait_recv()

        def add(rows, _):
            value = self.own(c, self.t, rows) + self.rx1[0, c, rows, :]
            for j in range(1, q):
                level = self.code_in[j, c, rows, :].astype(jnp.int32).astype(F32) + 32768.0
                value = value + level * (self.scale_in[j, c, 0:1, :] * (1.0 / 65535.0))
            self.final[rows, :] = value
            return 0

        self.loop(add)

    def finish(self, c):
        for j in range(self.n // 2):
            self.pair(c, j).wait_send()
            if j:
                self.chip(c, j, 0).wait_send()
                self.chip(c, j, 1).wait_send()


def scatter_scratch(n, slots, by, nz):
    q, rows = n // 2, by * UP
    return [
        pltpu.VMEM((slots, 2, rows, nz), F32),
        pltpu.VMEM((q, 2, rows, nz), F32),
        pltpu.VMEM((q, 2, rows, nz), F32),
        pltpu.VMEM((q, 2, rows, nz), jnp.int16),
        pltpu.VMEM((q, 2, 8, nz), F32),
        pltpu.VMEM((q, 2, rows, nz), jnp.int16),
        pltpu.VMEM((q, 2, 8, nz), F32),
        pltpu.VMEM((rows, nz), F32),
    ]


def scatter_sems(n):
    q = n // 2
    dma = pltpu.SemaphoreType.DMA
    return [dma((q, 2)), dma((q, 2)), dma((q, 2, 2)), dma((q, 2, 2))]


def update(c, bx, by, estimate, out, total, seen):
    def body(u, _):
        where = pl.ds(u * 2 * by + c, by, 2)
        out[where, :] = estimate[where, :] * total[pl.ds(u, by, UP), :] / seen
        return 0

    lax.fori_loop(0, bx, body, 0)


def round_wire(c, bx, by, estimate, wire):
    def body(y, _):
        for start, first in ((0, 0), (HB, bx - HB)):
            rows = estimate[pl.ds(first * 2 * by + 2 * y + c, HB, 2 * by), :]
            wire[c, y, start : start + HB, :] = rows.astype(BF16)
        return 0

    lax.fori_loop(0, by, body, 0)


def kernel(n, nv, dims, estimate, views, psf, background, bricks, slot_views, crossing, out, *scratch):
    taps, halo, bx, by, nz = dims
    slots = views.shape[0]
    take = lambda count: [scratch.pop(0) for _ in range(count)]
    scratch = list(scratch)
    (wire,), blocks, (seen_views, views_sem) = take(1), take(2), take(2)
    mats, (s1, s2, vf), parts = take(6), take(3), take(8)
    gather_all, scatter_all = take(7), take(4)
    g = Gather(n, nv, by, halo, wire, blocks, gather_all)
    f = Scatter(n, by, nz, bricks, *parts, scatter_all)
    factors = parts[0]

    def fetch(s):
        return pltpu.make_async_copy(views.at[s], seen_views.at[s], views_sem.at[s])

    round_wire(0, bx, by, estimate, wire)
    greet(n, nv, True)
    g.begin(0)
    for s in range(slots):
        fetch(s).start()
    round_wire(1, bx, by, estimate, wire)
    g.zeros()
    s2[...] = jnp.zeros_like(s2)
    vf[...] = jnp.zeros_like(vf)

    def bands(s, _):
        view = slot_views[s]
        build_bands(lambda a, k: psf[view, a, k], dims, [m.at[s] for m in mats])
        return 0

    lax.fori_loop(0, slots, bands, 0)
    g.forward(0)
    g.begin(1)
    g.forward_sides(0)
    g.arrive(0)

    def run(c, s):
        brick = bricks[s]
        if c == 0:
            fetch(s).wait()

        def emit(rows, value):
            factors[s, c, rows, :] = value

        line = 2 * (by + 2 * halo)

        def view(x, count):
            return seen_views[s, pl.ds(pl.multiple_of(x * line, 16), count * line), :]

        job(
            c,
            lambda y, count: blocks[c][pl.ds(brick * by + y, count)],
            view,
            background[slot_views[s]],
            dims,
            [m.at[s] for m in mats],
            s1,
            s2,
            vf,
            emit,
        )

    def beside(c, s):
        if c == 0:

            @pl.when(s == 0)
            def _():
                g.forward(1)

            @pl.when(s == 1)
            def _():
                g.forward_sides(1)

        else:

            @pl.when(s == 0)
            def _():
                f.send(0)

    for c in range(2):

        def step(s, _):
            run(c, s)
            beside(c, s)
            return 0

        lax.fori_loop(0, slots, step, 0)
        if c == 0:
            g.arrive(1)
        f.begin(c)
    seen = crossing[0]
    for k in range(1, crossing.shape[0]):
        seen = seen + crossing[k]
    seen = seen.astype(F32)
    f.total(0)
    update(0, bx, by, estimate, out, f.final, seen)
    f.send(1)
    for c in range(2):
        g.finish(c)
    f.total(1)
    update(1, bx, by, estimate, out, f.final, seen)
    for c in range(2):
        f.finish(c)


def on_device(n, nv, estimate, view_data, psf, background, slot_brick, slot_view, intersection):
    channels, bx, by, nz = estimate.shape
    taps = psf.shape[2]
    halo = taps // 2
    dims = (taps, halo, bx, by, nz)
    slots, px, py = slot_brick.shape[2], bx + 2 * halo, by + 2 * halo
    cells = jnp.transpose(estimate, (1, 2, 0, 3)).reshape(bx * by * channels, nz)
    views = jnp.transpose(view_data[0, 0], (0, 2, 3, 1, 4)).reshape(slots, px * py * channels, nz)
    count = 2 * halo + by * n + ROWS - py
    updated = pl.pallas_call(
        functools.partial(kernel, n, nv, dims),
        out_shape=jax.ShapeDtypeStruct(cells.shape, F32),
        in_specs=[VMEM, pl.BlockSpec(memory_space=pl.ANY)] + [SMEM] * 5,
        out_specs=VMEM,
        scratch_shapes=[pltpu.VMEM((channels, by, UP, nz), BF16)]
        + [pltpu.VMEM((count, ROWS, nz), BF16)] * 2
        + [pltpu.VMEM((slots, px * py * channels, nz), BF16), pltpu.SemaphoreType.DMA((slots,))]
        + job_scratch(slots, py, nz)
        + scatter_scratch(n, slots, by, nz)
        + gather_sems(n)
        + scatter_sems(n),
        compiler_params=pltpu.CompilerParams(
            collective_id=0, has_side_effects=True, vmem_limit_bytes=60 * 1024 * 1024
        ),
    )(
        cells,
        views,
        psf,
        background,
        slot_brick[0, 0],
        slot_view[0, 0],
        intersection[0, 0],
    )
    return jnp.transpose(updated.reshape(bx, by, channels, nz), (2, 0, 1, 3))


def solution(mesh):
    placed = (
        P(None, "view", "tile", None),
        P("view", "tile", None, None, None, None, None),
        P(),
        P(),
        P("view", "tile", None),
        P("view", "tile", None),
        P("view", "tile", None),
    )
    return jax.shard_map(
        functools.partial(on_device, mesh.shape["tile"], mesh.shape["view"]),
        mesh=mesh,
        in_specs=placed,
        out_specs=P(None, "view", "tile", None),
        check_vma=False,
    )
```

```python
import functools

import jax
import jax.numpy as jnp
from jax import lax
from jax.experimental import pallas as pl
from jax.experimental.pallas import tpu as pltpu
from jax.sharding import PartitionSpec as P

MESH = pl.DeviceIdType.MESH
F32 = jnp.float32
BF16 = jnp.bfloat16
ROWS = 64
HB = 16
UP = 32
PITCH1 = 72
PITCH2 = 40
GROUP = 10
VMEM = pl.BlockSpec(memory_space=pltpu.VMEM)
SMEM = pl.BlockSpec(memory_space=pltpu.SMEM)


def place(n):
    t, v = lax.axis_index("tile"), lax.axis_index("view")
    sib = t + 1 - 2 * lax.rem(t, 2)
    return t, v, sib


def same(t, step, n):
    return lax.rem(t + 2 * step + 2 * n, n)


def greet(n, nv, with_view):
    t, v, sib = place(n)
    barrier = pltpu.get_barrier_semaphore()

    def signal(tile, view):
        pl.semaphore_signal(barrier, inc=1, device_id=(tile, view), device_id_type=MESH)

    signal(sib, v)
    for k in range(1, n // 2):
        signal(same(t, k, n), v)
    peers = n // 2
    if with_view:

        @pl.when(v > 0)
        def _():
            signal(t, v - 1)

        @pl.when(v < nv - 1)
        def _():
            signal(t, v + 1)

        peers = peers + jnp.minimum(v, 1) + jnp.minimum(nv - 1 - v, 1)
    pl.semaphore_wait(barrier, peers)


class Gather:
    def __init__(self, n, nv, by, halo, wire, out, sems):
        self.n, self.nv, self.by, self.halo = n, nv, by, halo
        self.wire, self.out = wire, out
        self.sm, self.rm, self.sz, self.rz, self.ss, self.rs, self.loc = sems
        self.t, self.v, self.sib = place(n)

    def slab(self, c, b, part):
        start, size = ((HB, 2 * HB), (0, HB), (3 * HB, HB))[part]
        return self.out[c].at[pl.ds(self.halo + self.by * b, self.by), pl.ds(start, size), :]

    def copy(self, src, dst, s, r, dev):
        return pltpu.make_async_remote_copy(
            src_ref=src, dst_ref=dst, send_sem=s, recv_sem=r, device_id=dev, device_id_type=MESH
        )

    def main(self, c, k):
        return self.copy(
            self.wire.at[c],
            self.slab(c, self.t, 0),
            self.sm.at[c, k],
            self.rm.at[c, k],
            (same(self.t, k, self.n), self.v),
        )

    def to_sib(self, c, k, part):
        b = same(self.t, -k, self.n)
        src = self.wire.at[c] if (k == 0 and part == 0) else self.slab(c, b, part)
        return self.copy(
            src, self.slab(c, b, part), self.ss.at[c, k, part], self.rs.at[c, k, part], (self.sib, self.v)
        )

    def to_view(self, c, k, up):
        b = same(self.t, -k, self.n)
        first = HB if up else 0
        if k == 0:
            src = self.wire.at[c, :, pl.ds(first, HB), :]
        else:
            src = self.out[c].at[pl.ds(self.halo + self.by * b, self.by), pl.ds(HB + first, HB), :]
        side = 0 if up else 1
        return self.copy(
            src,
            self.slab(c, b, 1 if up else 2),
            self.sz.at[c, k, side],
            self.rz.at[c, k, side],
            (self.t, self.v + 1 if up else self.v - 1),
        )

    def local(self, c):
        return pltpu.make_async_copy(self.wire.at[c], self.slab(c, self.t, 0), self.loc.at[c])

    def views(self, c, k, act):
        @pl.when(self.v < self.nv - 1)
        def _():
            act(self.to_view(c, k, True))

        @pl.when(self.v > 0)
        def _():
            act(self.to_view(c, k, False))

    def zeros(self):
        count = self.out[0].shape[0]
        last = self.halo + self.by * self.n

        def fill(low, high, start, size):
            def body(i, _):
                for ref in self.out:
                    ref[pl.ds(i, 1), pl.ds(start, size), :] = jnp.zeros((1, size, ref.shape[2]), BF16)
                return 0

            lax.fori_loop(low, high, body, 0)

        fill(0, self.halo, 0, ROWS)
        fill(last, count, 0, ROWS)

        @pl.when(self.v == 0)
        def _():
            fill(self.halo, last, 0, HB)

        @pl.when(self.v == self.nv - 1)
        def _():
            fill(self.halo, last, 3 * HB, HB)

    def begin(self, c):
        for k in range(1, self.n // 2):
            self.main(c, k).start()
        self.views(c, 0, lambda d: d.start())
        self.to_sib(c, 0, 0).start()
        self.local(c).start()

    def forward(self, c):
        for k in range(1, self.n // 2):
            self.main(c, k).wait_recv()
            self.views(c, k, lambda d: d.start())
            self.to_sib(c, k, 0).start()

    def forward_sides(self, c):
        def side(k, part, when):
            @pl.when(when)
            def _():
                self.to_view(c, k, part == 1).wait_recv()
                self.to_sib(c, k, part).start()

        for k in range(self.n // 2):
            side(k, 1, self.v > 0)
            side(k, 2, self.v < self.nv - 1)

    def arrive(self, c):
        self.local(c).wait()
        for k in range(self.n // 2):
            self.to_sib(c, k, 0).wait_recv()

            @pl.when(self.v > 0)
            def _():
                self.to_sib(c, k, 1).wait_recv()

            @pl.when(self.v < self.nv - 1)
            def _():
                self.to_sib(c, k, 2).wait_recv()

    def finish(self, c):
        for k in range(self.n // 2):
            if k:
                self.main(c, k).wait_send()
            self.views(c, k, lambda d: d.wait_send())
            self.to_sib(c, k, 0).wait_send()

            @pl.when(self.v > 0)
            def _():
                self.to_sib(c, k, 1).wait_send()

            @pl.when(self.v < self.nv - 1)
            def _():
                self.to_sib(c, k, 2).wait_send()


def gather_sems(n):
    q = n // 2
    dma = pltpu.SemaphoreType.DMA
    return [dma((2, q)), dma((2, q)), dma((2, q, 2)), dma((2, q, 2)), dma((2, q, 3)), dma((2, q, 3)), dma((2,))]


def iota(shape, dim):
    return lax.broadcasted_iota(jnp.int32, shape, dim)


def split(x):
    hi = x.astype(BF16)
    return hi, (x - hi.astype(F32)).astype(BF16)


def band(tap, count, index, valid):
    index = jnp.where(valid, index, -1)
    total = jnp.zeros(index.shape, F32)
    for k in range(count):
        total = jnp.where(index == k, tap(k), total)
    return total


def build_bands(tap, dims, mats):
    fx, fy, cx, cy, fz, cz = mats
    taps, halo, bx, by, nz = dims
    px, py = bx + 2 * halo, by + 2 * halo

    def keep(ref, value):
        ref[...] = jnp.concatenate(split(value), axis=0)

    p, col = iota((ROWS, 2 * ROWS), 0), iota((ROWS, 2 * ROWS), 1)
    r = jnp.where(col >= ROWS, col - ROWS, col)
    gap = 2 * HB - (bx - HB) + HB
    x = jnp.where(r < 2 * HB, r - HB, r - gap + HB)
    fresh = (r < 2 * HB) | (x >= HB)
    q = x + halo
    valid = fresh & (q >= 0) & (q < px) & (p < px)
    keep(fx, band(lambda k: tap(0, k), taps, q - p + halo, valid)[:, :ROWS])
    keep(fy, band(lambda k: tap(1, k), taps, r - p + halo, (r < py) & (p < py)))
    p, r = p[:UP], r[:UP]
    keep(cx, band(lambda k: tap(0, k), taps, p - r + 2 * halo, (r < px) & (p < bx)))
    keep(cy, band(lambda k: tap(1, k), taps, p - r + 2 * halo, (r < py) & (p < by)))
    z, w = iota((nz, nz), 0), iota((nz, nz), 1)
    for ref, offset in ((fz, z - w), (cz, w - z)):
        both = jnp.concatenate(split(band(lambda k: tap(2, k), taps, offset + halo, w < nz)), axis=1)
        ref[...] = jnp.concatenate([both, both], axis=0)


def dot(a, b):
    return jnp.dot(a, b, preferred_element_type=F32)


def along(mat, a, b):
    both = jnp.concatenate([a, b], axis=1)
    if both.dtype != BF16:
        both = jnp.concatenate(split(both), axis=0)
    out = dot(mat[...], both)
    half = out.shape[0] // 2
    return out[:half] + out[half:]


def along_last(x, mat):
    out = dot(jnp.concatenate(split(x), axis=1), mat[...])
    half = out.shape[1] // 2
    return out[:, :half] + out[:, half:]


def apart(pairs, nz):
    return jnp.concatenate([v for f in pairs for v in (f[:, :nz], f[:, nz:])], axis=0)


def in_groups(count, size, body):
    full = count // size
    if full:

        def step(i, _):
            body(i * size, size)
            return 0

        lax.fori_loop(0, full, step, 0)
    if count % size:
        body(full * size, count % size)


def staged(items, stages):
    held = [stages[0](i) for i in items]
    for stage in stages[1:]:
        held = [stage(i, h) for i, h in zip(items, held)]


def job(c, block, view, backdrop, dims, mats, s1, s2, vf, emit):
    fx, fy, cx, cy, fz, cz = mats
    taps, halo, bx, by, nz = dims
    px, py = bx + 2 * halo, by + 2 * halo

    def put(ref, line, pitch, size, value):
        ref[pl.ds(pl.multiple_of(line * pitch, 8), size), :] = value[:, :nz]
        ref[pl.ds(pl.multiple_of((line + 1) * pitch, 8), size), :] = value[:, nz:]

    def first(y, count):
        e = block(y, count)
        part = count

        def ahead(k):
            return apart([along(fx, e[j], e[j + 1]) for j in range(k, k + part, 2)], nz)

        def after(k, u):
            t = along_last(u, fz)
            for j in range(part):
                s1[pl.ds(pl.multiple_of((y + k + j) * PITCH1, 8), ROWS), :] = t[j * ROWS : (j + 1) * ROWS]

        staged(range(0, count, part), [ahead, after])

    in_groups(ROWS, 16, first)

    def second(pair, count):
        line = 2 * py
        vf[: count * 2 * line, :] = view(2 * pair, 2 * count).astype(F32)

        def forward(j):
            x = 2 * (pair + j)
            return along(fy, s1[pl.ds(x, ROWS, PITCH1), :], s1[pl.ds(x + 1, ROWS, PITCH1), :])

        def ratio(j, blurred):
            predicted = blurred + backdrop
            va = vf[pl.ds(2 * j * line + c, ROWS, 2), :]
            vb = vf[pl.ds((2 * j + 1) * line + c, ROWS, 2), :]
            return va / predicted[:, :nz], vb / predicted[:, nz:]

        def back(j, lines):
            put(s2, 2 * (pair + j), PITCH2, UP, along(cy, *lines))

        staged(range(count), [forward, ratio, back])

    in_groups(px // 2, GROUP, second)

    def third(pair, count):
        part = count

        def ahead(k):
            lines = []
            for j in range(k, min(k + part, count)):
                y = 2 * (pair + j)
                lines.append(along(cx, s2[pl.ds(y, ROWS, PITCH2), :], s2[pl.ds(y + 1, ROWS, PITCH2), :]))
            return apart(lines, nz)

        def after(k, f):
            emit(pl.ds(pl.multiple_of((pair + k) * 2 * UP, 8), f.shape[0]), along_last(f, cz))

        staged(range(0, count, part), [ahead, after])

    in_groups(by // 2, 14, third)


def job_scratch(slots, py, nz):
    return [
        pltpu.VMEM((slots, 2 * ROWS, ROWS), BF16),
        pltpu.VMEM((slots, 2 * ROWS, 2 * ROWS), BF16),
        pltpu.VMEM((slots, 2 * UP, 2 * ROWS), BF16),
        pltpu.VMEM((slots, 2 * UP, 2 * ROWS), BF16),
        pltpu.VMEM((slots, 2 * nz, 2 * nz), BF16),
        pltpu.VMEM((slots, 2 * nz, 2 * nz), BF16),
        pltpu.VMEM((ROWS * PITCH1, nz), F32),
        pltpu.VMEM((ROWS * PITCH2, nz), F32),
        pltpu.VMEM((GROUP * 4 * py + 16, nz), F32),
    ]


class Scatter:
    def __init__(self, n, by, nz, bricks, factors, tx1, rx1, code, scale, code_in, scale_in, final, sems):
        self.n, self.nz, self.rows = n, nz, by * UP
        self.bricks, self.factors, self.tx1, self.rx1, self.final = bricks, factors, tx1, rx1, final
        self.code, self.scale, self.code_in, self.scale_in = code, scale, code_in, scale_in
        self.s1, self.r1, self.s2, self.r2 = sems
        self.t, self.v, self.sib = place(n)

    def own(self, c, o, rows):
        parts = [
            jnp.where(self.bricks[s] == o, self.factors[s, c, rows, :], 0.0)
            for s in range(self.factors.shape[0])
        ]
        return sum(parts[1:], parts[0])

    def loop(self, body, init=0):
        piece = 128

        def step(i, carry):
            return body(pl.ds(pl.multiple_of(i * piece, 16), piece), carry)

        return lax.fori_loop(0, self.rows // piece, step, init)

    def pair(self, c, j):
        return pltpu.make_async_remote_copy(
            src_ref=self.tx1.at[j, c],
            dst_ref=self.rx1.at[j, c],
            send_sem=self.s1.at[j, c],
            recv_sem=self.r1.at[j, c],
            device_id=(self.sib, self.v),
            device_id_type=MESH,
        )

    def chip(self, c, j, kind):
        src, dst = ((self.code, self.code_in), (self.scale, self.scale_in))[kind]
        return pltpu.make_async_remote_copy(
            src_ref=src.at[j, c],
            dst_ref=dst.at[j, c],
            send_sem=self.s2.at[j, c, kind],
            recv_sem=self.r2.at[j, c, kind],
            device_id=(same(self.t, j, self.n), self.v),
            device_id_type=MESH,
        )

    def begin(self, c):
        for j in list(range(1, self.n // 2)) + [0]:
            o = same(self.sib, j, self.n)

            def fill(rows, _):
                self.tx1[j, c, rows, :] = self.own(c, o, rows)
                return 0

            self.loop(fill)
            self.pair(c, j).start()

    def send(self, c):
        for j in range(1, self.n // 2):
            self.pair(c, j).wait_recv()
            o = same(self.t, j, self.n)

            def add(rows, top):
                value = self.own(c, o, rows) + self.rx1[j, c, rows, :]
                self.rx1[j, c, rows, :] = value
                return jnp.maximum(top, jnp.max(value.reshape(-1, 8, self.nz), axis=0))

            top = self.loop(add, jnp.zeros((8, self.nz), F32))
            top = jnp.max(top, axis=0, keepdims=True)
            top = jnp.where(top > 0.0, top, 1.0)
            self.scale[j, c] = jnp.broadcast_to(top, (8, self.nz))
            gain = 1.0 / top

            def pack(rows, _):
                level = jnp.minimum(self.rx1[j, c, rows, :] * gain * 65535.0, 65535.0)
                whole = jnp.round(level).astype(jnp.int32) - 32768
                self.code[j, c, rows, :] = whole.astype(jnp.int16)
                return 0

            self.loop(pack)
            self.chip(c, j, 0).start()
            self.chip(c, j, 1).start()

    def total(self, c):
        q = self.n // 2
        self.pair(c, 0).wait_recv()
        for j in range(1, q):
            self.chip(c, j, 0).wait_recv()
            self.chip(c, j, 1).wait_recv()

        def add(rows, _):
            value = self.own(c, self.t, rows) + self.rx1[0, c, rows, :]
            for j in range(1, q):
                level = self.code_in[j, c, rows, :].astype(jnp.int32).astype(F32) + 32768.0
                value = value + level * (self.scale_in[j, c, 0:1, :] * (1.0 / 65535.0))
            self.final[rows, :] = value
            return 0

        self.loop(add)

    def finish(self, c):
        for j in range(self.n // 2):
            self.pair(c, j).wait_send()
            if j:
                self.chip(c, j, 0).wait_send()
                self.chip(c, j, 1).wait_send()


def scatter_scratch(n, slots, by, nz):
    q, rows = n // 2, by * UP
    return [
        pltpu.VMEM((slots, 2, rows, nz), F32),
        pltpu.VMEM((q, 2, rows, nz), F32),
        pltpu.VMEM((q, 2, rows, nz), F32),
        pltpu.VMEM((q, 2, rows, nz), jnp.int16),
        pltpu.VMEM((q, 2, 8, nz), F32),
        pltpu.VMEM((q, 2, rows, nz), jnp.int16),
        pltpu.VMEM((q, 2, 8, nz), F32),
        pltpu.VMEM((rows, nz), F32),
    ]


def scatter_sems(n):
    q = n // 2
    dma = pltpu.SemaphoreType.DMA
    return [dma((q, 2)), dma((q, 2)), dma((q, 2, 2)), dma((q, 2, 2))]


def update(c, bx, by, estimate, out, total, seen):
    def body(u, _):
        where = pl.ds(u * 2 * by + c, by, 2)
        out[where, :] = estimate[where, :] * total[pl.ds(u, by, UP), :] / seen
        return 0

    lax.fori_loop(0, bx, body, 0)


def round_wire(c, bx, by, estimate, wire):
    def body(y, _):
        for start, first in ((0, 0), (HB, bx - HB)):
            rows = estimate[pl.ds(first * 2 * by + 2 * y + c, HB, 2 * by), :]
            wire[c, y, start : start + HB, :] = rows.astype(BF16)
        return 0

    lax.fori_loop(0, by, body, 0)


def kernel(n, nv, dims, estimate, views, psf, background, bricks, slot_views, crossing, out, *scratch):
    taps, halo, bx, by, nz = dims
    slots = views.shape[0]
    take = lambda count: [scratch.pop(0) for _ in range(count)]
    scratch = list(scratch)
    (wire,), blocks, (seen_views, views_sem) = take(1), take(2), take(2)
    mats, (s1, s2, vf), parts = take(6), take(3), take(8)
    gather_all, scatter_all = take(7), take(4)
    g = Gather(n, nv, by, halo, wire, blocks, gather_all)
    f = Scatter(n, by, nz, bricks, *parts, scatter_all)
    factors = parts[0]

    def fetch(s):
        return pltpu.make_async_copy(views.at[s], seen_views.at[s], views_sem.at[s])

    round_wire(0, bx, by, estimate, wire)
    greet(n, nv, True)
    g.begin(0)
    for s in range(slots):
        fetch(s).start()
    round_wire(1, bx, by, estimate, wire)
    g.zeros()
    s2[...] = jnp.zeros_like(s2)
    vf[...] = jnp.zeros_like(vf)

    def bands(s, _):
        view = slot_views[s]
        build_bands(lambda a, k: psf[view, a, k], dims, [m.at[s] for m in mats])
        return 0

    lax.fori_loop(0, slots, bands, 0)
    g.forward(0)
    g.begin(1)
    g.forward_sides(0)
    g.arrive(0)

    def run(c, s):
        brick = bricks[s]
        if c == 0:
            fetch(s).wait()

        def emit(rows, value):
            factors[s, c, rows, :] = value

        line = 2 * (by + 2 * halo)

        def view(x, count):
            return seen_views[s, pl.ds(pl.multiple_of(x * line, 16), count * line), :]

        job(
            c,
            lambda y, count: blocks[c][pl.ds(brick * by + y, count)],
            view,
            background[slot_views[s]],
            dims,
            [m.at[s] for m in mats],
            s1,
            s2,
            vf,
            emit,
        )

    def beside(c, s):
        if c == 0:

            @pl.when(s == 0)
            def _():
                g.forward(1)

            @pl.when(s == 1)
            def _():
                g.forward_sides(1)

        else:

            @pl.when(s == 0)
            def _():
                f.send(0)

    for c in range(2):

        def step(s, _):
            run(c, s)
            beside(c, s)
            return 0

        lax.fori_loop(0, slots, step, 0)
        if c == 0:
            g.arrive(1)
        f.begin(c)
    seen = crossing[0]
    for k in range(1, crossing.shape[0]):
        seen = seen + crossing[k]
    seen = seen.astype(F32)
    f.total(0)
    update(0, bx, by, estimate, out, f.final, seen)
    f.send(1)
    for c in range(2):
        g.finish(c)
    f.total(1)
    update(1, bx, by, estimate, out, f.final, seen)
    for c in range(2):
        f.finish(c)


def on_device(n, nv, estimate, view_data, psf, background, slot_brick, slot_view, intersection):
    channels, bx, by, nz = estimate.shape
    taps = psf.shape[2]
    halo = taps // 2
    dims = (taps, halo, bx, by, nz)
    slots, px, py = slot_brick.shape[2], bx + 2 * halo, by + 2 * halo
    cells = jnp.transpose(estimate, (1, 2, 0, 3)).reshape(bx * by * channels, nz)
    views = jnp.transpose(view_data[0, 0], (0, 2, 3, 1, 4)).reshape(slots, px * py * channels, nz)
    count = 2 * halo + by * n + ROWS - py
    updated = pl.pallas_call(
        functools.partial(kernel, n, nv, dims),
        out_shape=jax.ShapeDtypeStruct(cells.shape, F32),
        in_specs=[VMEM, pl.BlockSpec(memory_space=pl.ANY)] + [SMEM] * 5,
        out_specs=VMEM,
        scratch_shapes=[pltpu.VMEM((channels, by, UP, nz), BF16)]
        + [pltpu.VMEM((count, ROWS, nz), BF16)] * 2
        + [pltpu.VMEM((slots, px * py * channels, nz), BF16), pltpu.SemaphoreType.DMA((slots,))]
        + job_scratch(slots, py, nz)
        + scatter_scratch(n, slots, by, nz)
        + gather_sems(n)
        + scatter_sems(n),
        compiler_params=pltpu.CompilerParams(
            collective_id=0, has_side_effects=True, vmem_limit_bytes=60 * 1024 * 1024
        ),
    )(
        cells,
        views,
        psf,
        background,
        slot_brick[0, 0],
        slot_view[0, 0],
        intersection[0, 0],
    )
    return jnp.transpose(updated.reshape(bx, by, channels, nz), (2, 0, 1, 3))


def solution(mesh):
    placed = (
        P(None, "view", "tile", None),
        P("view", "tile", None, None, None, None, None),
        P(),
        P(),
        P("view", "tile", None),
        P("view", "tile", None),
        P("view", "tile", None),
    )
    return jax.shard_map(
        functools.partial(on_device, mesh.shape["tile"], mesh.shape["view"]),
        mesh=mesh,
        in_specs=placed,
        out_specs=P(None, "view", "tile", None),
        check_vma=False,
    )
```
